256 devices in a mesh: fsdp: 64 (over z, x_lo, y), tp: 4 (over x_hi, core).
Axes of the slice: x: 4 (x_hi: 2, x_lo: 2; x = x_hi * 2 + x_lo), y: 4, z: 8, core: 2. Of those that a mesh axis runs over, the one named last changes fastest.
Arguments:
- tokens: bfloat16 [65536, 5120], P('fsdp', 'tp'), may hold values from -16 to 16
- grad_out: bfloat16 [65536, 2, 1024], P('fsdp', None, 'tp'), may hold values from -700 to 700, as said below
- weight: float32 [5120, 2, 1024], P('fsdp', None, 'tp'), may hold values from -0.009765625 to 0.009765625
- moment_one: float32 [5120, 2, 1024], P('fsdp', None, 'tp'), may hold values from -0.00061035156 to 0.00061035156
- moment_two: float32 [5120, 2, 1024], P('fsdp', None, 'tp'), may hold values from 1e-09 to 1e-07
- rollout_hidden: bfloat16 [256, 4, 5120], P('fsdp'), may hold values from -6 to 6
- queries: bfloat16 [256, 4, 8192], P('fsdp', None, 'tp'), may hold values from -160 to 160
- cache_keys: bfloat16 [256, 2048, 1024], P('fsdp', None, 'tp'), may hold values from -5 to 5
- cache_values: bfloat16 [256, 2048, 1024], P('fsdp', None, 'tp'), may hold values from -6 to 6
- cache_lengths: int32 [256], P('fsdp'), may hold values from 256 to 2048, as said below
- key_gain: float32 [128], replicated, may hold values from 0.1 to 1.9
Outputs:
- new_weight: float32 [5120, 2, 1024], P('fsdp', None, 'tp')
- adam_step: float32 [5120, 2, 1024], P('fsdp', None, 'tp')
- new_keys: bfloat16 [256, 4, 1024], P('fsdp', None, 'tp')
- new_values: bfloat16 [256, 4, 1024], P('fsdp', None, 'tp')
- attended: bfloat16 [256, 4, 8192], P('fsdp', None, 'tp')
The draws below stay inside these ranges and needn't reach their ends.
Inputs may be any that keep to these rules, and one draw needn't show every extreme that they name: `grad_out`: real values; the first row's ramp across the tokens and the spread across columns make every scale of order one to ten. `cache_lengths`: at least one row has exactly 2048 filled slots; every row has at least 256.
All inputs are finite; a program needn't handle non-finite values.
Results may differ from the reference program's by a relative error of at most 0.0049.
Values may be sent and summed in bfloat16 or wider, within the bound.
No kernel may reach another device: no remote copies, remote signals or barrier semaphores. Data moves between devices by JAX's collectives and lax.ppermute only.
A program may use at most 128 MiB of HBM per device.

```python
import math
import jax
import jax.numpy as jnp
from jax import lax

D = 5120
QH = 64
KVH = 8
HD = 128
STEPS = 4
CACHE = 2048
KVC = 1024
TOKENS = 65536
ROWS = 256


def cache_front(key):
    return jnp.clip(jax.random.normal(key, (ROWS, 2, KVC), jnp.float32), -5.0, 5.0)


def draw_grad_out(key, part):
    key = jax.random.fold_in(key, 11)
    key_list = jax.random.split(key, 2)
    row_ramp = 1.0 + 2.0 * jnp.arange(TOKENS, dtype=jnp.float32) / TOKENS
    column_scale = jnp.exp(jax.random.uniform(key_list[1], (1, 2, KVC), jnp.float32) * jnp.log(10.0))
    noise_part = jnp.clip(jax.random.normal(key_list[0], (TOKENS, 2, KVC), jnp.float32), -5.0, 5.0)
    values = noise_part * row_ramp[:, None, None] * column_scale
    return values.astype(jnp.bfloat16)


def draw_cache_lengths(key, part):
    key = jax.random.fold_in(key, 12)
    key_list = jax.random.split(key, 2)
    lengths = jax.random.randint(key_list[0], (ROWS,), CACHE // 8, CACHE + 1)
    chosen = jax.random.randint(key_list[1], (), 0, ROWS)
    return jnp.where(jnp.arange(ROWS) == chosen, CACHE, lengths).astype(jnp.int32)


def draw_cache_keys(key, part):
    front = cache_front(key)
    key = jax.random.fold_in(key, 13)
    remainder = jnp.clip(jax.random.normal(key, (ROWS, CACHE - 2, KVC), jnp.float32), -5.0, 5.0)
    return jnp.concatenate([front, remainder], axis=1).astype(jnp.bfloat16)


def draw_queries(key, part):
    key = jax.random.fold_in(key, 14)
    values = jnp.clip(jax.random.normal(key, (ROWS, STEPS, QH * HD), jnp.float32), -5.0, 5.0)
    return values.astype(jnp.bfloat16)


def spiked(entries, own_key, source, target, blocks, factor):
    def block_of(position):
        return (jnp.arange(entries.shape[position]) // (entries.shape[position] // blocks)).reshape((-1,) + (1,) * (entries.ndim - 1 - position))

    near = jax.random.permutation(own_key, blocks)[block_of(target)]
    other_side = (block_of(target) + blocks // 2) % blocks
    return jnp.where((block_of(source) == near) | (block_of(source) == other_side), factor * entries, entries)


def levels(key, shape, cuts, smallest, top_value):
    level, own = 1.0, jax.random.fold_in(key, 6)
    for axis_at, shards_of in cuts:
        draws = jnp.exp(jax.random.uniform(jax.random.fold_in(own, axis_at), (shards_of,), jnp.float32, smallest / len(cuts), top_value / len(cuts)))
        level = level * jnp.repeat(draws, shape[axis_at] // shards_of).reshape([-1 if axis == axis_at else 1 for axis in range(len(shape))])
    return level


def noise(own_key, dims, deviation, bound, cuts=(), kind=jnp.bfloat16):
    factor_of = levels(own_key, dims, cuts, -0.22, 0.18) if cuts else 1.0
    values = jax.random.normal(own_key, dims, jnp.float32) * deviation * factor_of
    return jnp.minimum(jnp.maximum(values, -bound), bound).astype(kind)


def gaussian_with(rng, dims, width, bound, cuts, heavy, kind=jnp.bfloat16):
    result = width * jax.random.normal(rng, dims, jnp.float32)
    if cuts:
        result = result * levels(rng, dims, cuts, -0.22, 0.18)
    return jnp.clip(spiked(result, jax.random.fold_in(rng, 3), *heavy), -bound, bound).astype(kind)


def setup_inputs(seed: int = 0) -> dict:
    seeds = jax.random.split(jax.random.key(seed), 12)
    return {
        "tokens": gaussian_with(seeds[0], (TOKENS, D), 1.0, 16.0, ((0, 64), (1, 4)), (0, 1, 64, 4.0)),
        "grad_out": draw_grad_out(jax.random.fold_in(seeds[11], 71), 0),
        "weight": noise(seeds[2], (D, 2, KVC), (64 * D) ** -0.5, 0.009765625, ((0, 64), (2, 4)), jnp.float32),
        "moment_one": noise(seeds[3], (D, 2, KVC), 0.0001, 0.00061035156, ((0, 64), (2, 4)), jnp.float32),
        "moment_two": jnp.clip(jnp.exp(math.log(1.0000000116860974e-07) - 4.6051702 * jax.random.uniform(seeds[4], (D, 2, KVC), jnp.float32) ** levels(seeds[4], (D, 2, KVC), ((0, 64), (2, 4)), -0.2, 0.2)), 9.999999717180685e-10, 1.0000000116860974e-07),
        "rollout_hidden": noise(seeds[5], (ROWS, STEPS, D), 1.0, 6.0, ((0, 64),)),
        "queries": draw_queries(jax.random.fold_in(seeds[11], 71), 0),
        "cache_keys": draw_cache_keys(jax.random.fold_in(seeds[11], 71), 0),
        "cache_values": noise(seeds[8], (ROWS, CACHE, KVC), 1.0, 6.0, ((0, 64), (2, 4))),
        "cache_lengths": draw_cache_lengths(jax.random.fold_in(seeds[11], 71), 0),
        "key_gain": jnp.clip(1.0 + 0.18 * jax.random.normal(seeds[10], (HD,), jnp.float32), 0.1, 1.9),
    }


beta_one = 0.9
beta_two = 0.999
learn_rate = 0.001
decay_rate = 0.1
adam_eps = 1e-08
step_number = 10.0
clip_rms = 0.001
norm_eps = 1e-06
rope_base = 1000000.0

def adamw_update(weight, gradient, moment_one, moment_two, factor):
    clipped = gradient * factor
    first_moment = beta_one * moment_one + (1.0 - beta_one) * clipped
    second_moment = beta_two * moment_two + (1.0 - beta_two) * clipped * clipped
    first_hat = first_moment / (1.0 - beta_one ** step_number)
    second_hat = second_moment / (1.0 - beta_two ** step_number)
    direction = first_hat / (jnp.sqrt(second_hat) + adam_eps) + decay_rate * weight
    return (weight - learn_rate * direction, direction)

def rotate_keys(values, positions):
    half_width = values.shape[-1] // 2
    frequency = rope_base ** (-2.0 * jnp.arange(half_width, dtype=jnp.float32) / values.shape[-1])
    angles = positions.astype(jnp.float32)[..., None] * frequency
    cosine = jnp.cos(angles)
    sine_part = jnp.sin(angles)
    first_half = values[..., :half_width]
    second_half = values[..., half_width:]
    return jnp.concatenate([first_half * cosine - second_half * sine_part, second_half * cosine + first_half * sine_part], axis=-1)

def norm_keys(raw_keys, key_gain):
    return raw_keys * lax.rsqrt(lax.optimization_barrier(jnp.mean(raw_keys * raw_keys, axis=-1, keepdims=True)) + norm_eps) * key_gain

def attend_row(row_item):
    query_row, cache_key_row, cache_value_row, key_row, value_row, length = row_item
    groups = QH // KVH
    query_heads = query_row.astype(jnp.float32).reshape(STEPS, KVH, groups, HD)
    old_keys = cache_key_row.astype(jnp.float32).reshape(CACHE, KVH, HD)
    old_values = cache_value_row.astype(jnp.float32).reshape(CACHE, KVH, HD)
    fresh_keys = key_row.astype(jnp.float32).reshape(STEPS, KVH, HD)
    fresh_values = value_row.astype(jnp.float32).reshape(STEPS, KVH, HD)
    scale_factor = 1.0 / math.sqrt(HD)
    old_scores = jnp.einsum('sgqd,cgd->gqsc', query_heads, old_keys) * scale_factor
    fresh_scores = jnp.einsum('sgqd,tgd->gqst', query_heads, fresh_keys) * scale_factor
    old_valid = jnp.arange(CACHE, dtype=jnp.int32) < length
    fresh_valid = jnp.arange(STEPS)[:, None] >= jnp.arange(STEPS)[None, :]
    old_scores = jnp.where(old_valid, old_scores, -jnp.inf)
    fresh_scores = jnp.where(fresh_valid, fresh_scores, -jnp.inf)
    top_score = jnp.maximum(lax.optimization_barrier(jnp.max(old_scores, axis=-1, keepdims=True)), lax.optimization_barrier(jnp.max(fresh_scores, axis=-1, keepdims=True)))
    old_exp = jnp.exp(old_scores - top_score)
    fresh_exp = jnp.exp(fresh_scores - top_score)
    denominator = lax.optimization_barrier(jnp.sum(old_exp, axis=-1, keepdims=True)) + lax.optimization_barrier(jnp.sum(fresh_exp, axis=-1, keepdims=True))
    old_weights = lax.optimization_barrier((old_exp / denominator).astype(jnp.bfloat16)).astype(jnp.float32)
    fresh_weights = lax.optimization_barrier((fresh_exp / denominator).astype(jnp.bfloat16)).astype(jnp.float32)
    mixed = jnp.einsum('gqsc,cgd->sgqd', old_weights, old_values) + jnp.einsum('gqst,tgd->sgqd', fresh_weights, fresh_values)
    return mixed.astype(jnp.bfloat16).reshape(STEPS, QH * HD)

def reference(tokens, grad_out, weight, moment_one, moment_two, rollout_hidden, queries, cache_keys, cache_values, cache_lengths, key_gain):
    gradient = jnp.dot(tokens.T, grad_out.reshape(TOKENS, 2 * KVC), preferred_element_type=jnp.float32) / TOKENS
    squares = jnp.sum(gradient * gradient)
    factor = jnp.minimum(1.0, clip_rms / jnp.sqrt(squares / (2.0 * D * KVC) + norm_eps))
    new_weight, adam_step = adamw_update(weight.reshape(D, 2 * KVC), gradient, moment_one.reshape(D, 2 * KVC), moment_two.reshape(D, 2 * KVC), factor)
    rollout_weight = new_weight.astype(jnp.bfloat16)
    projected = jnp.dot(rollout_hidden.reshape(ROWS * STEPS, D), rollout_weight, preferred_element_type=jnp.float32)
    projected = projected.reshape(ROWS, STEPS, 2, KVH, HD)
    positions = cache_lengths[:, None] + jnp.arange(STEPS, dtype=jnp.int32)[None, :]
    new_keys = rotate_keys(norm_keys(projected[:, :, 0], key_gain), positions[:, :, None]).astype(jnp.bfloat16).reshape(ROWS, STEPS, KVC)
    new_values = projected[:, :, 1].astype(jnp.bfloat16).reshape(ROWS, STEPS, KVC)
    attended = lax.map(attend_row, (queries, cache_keys, cache_values, new_keys, new_values, cache_lengths))
    return (new_weight.reshape(D, 2, KVC), adam_step.reshape(D, 2, KVC), new_keys, new_values, attended)
```

```python
import functools
import math

import jax
import jax.numpy as jnp
from jax import lax
from jax.experimental import pallas as pl
from jax.experimental.pallas import tpu as pltpu
from jax.sharding import Mesh
from jax.sharding import PartitionSpec as P

QH = 64
KVH = 8
HD = 128

beta_one = 0.9
beta_two = 0.999
learn_rate = 0.001
decay_rate = 0.1
adam_eps = 1e-08
step_number = 10.0
clip_rms = 0.001
norm_eps = 1e-06
rope_base = 1000000.0

SIZES = {"z": 8, "xl": 2, "y": 4, "xh": 2, "core": 2}
FSDP = ("z", "xl", "y")
TP = ("xh", "core")
EVERY = FSDP + TP

BF16 = jnp.bfloat16
F32 = jnp.float32


def adamw_update(weight, gradient, moment_one, moment_two, factor):
    clipped = gradient * factor
    first_moment = beta_one * moment_one + (1.0 - beta_one) * clipped
    second_moment = beta_two * moment_two + (1.0 - beta_two) * clipped * clipped
    first_hat = first_moment / (1.0 - beta_one**step_number)
    second_hat = second_moment / (1.0 - beta_two**step_number)
    direction = first_hat / (jnp.sqrt(second_hat) + adam_eps) + decay_rate * weight
    return (weight - learn_rate * direction, direction)


def rotate_keys(values, positions):
    half_width = values.shape[-1] // 2
    frequency = rope_base ** (-2.0 * jnp.arange(half_width, dtype=F32) / values.shape[-1])
    angles = positions.astype(F32)[..., None] * frequency
    cosine = jnp.cos(angles)
    sine_part = jnp.sin(angles)
    first_half = values[..., :half_width]
    second_half = values[..., half_width:]
    return jnp.concatenate(
        [
            first_half * cosine - second_half * sine_part,
            second_half * cosine + first_half * sine_part,
        ],
        axis=-1,
    )


def norm_keys(raw_keys, key_gain):
    return (
        raw_keys
        * lax.rsqrt(jnp.mean(raw_keys * raw_keys, axis=-1, keepdims=True) + norm_eps)
        * key_gain
    )


def swap(values, axis):
    return lax.ppermute(values, axis, [(0, 1), (1, 0)])


PAIRING = ([(0, 1), (1, 0), (2, 3), (3, 2)], [(0, 3), (3, 0), (1, 2), (2, 1)])


def partner(position, pairing):
    return position ^ 1 if pairing == 0 else 3 - position


def at_y(block, position):
    return lax.dynamic_index_in_dim(block, position, axis=2, keepdims=False)


def reduce_y(block, first):
    second = 1 - first
    me = lax.axis_index("y")
    far = partner(me, first)
    away = jnp.stack([at_y(block, partner(far, second)), at_y(block, far)])
    got = lax.ppermute(away, "y", PAIRING[first])
    near = partner(me, second)
    passed = (at_y(block, near).astype(F32) + got[0].astype(F32)).astype(BF16)
    last = lax.ppermute(passed, "y", PAIRING[second])
    return at_y(block, me).astype(F32) + got[1].astype(F32) + last.astype(F32)


def old_attention_kernel(length_ref, query_ref, key_ref, value_ref, out_ref, top_ref, total_ref):
    length = length_ref[pl.program_id(0)]
    scores = lax.dot_general(
        query_ref[0, 0], key_ref[0], (((1,), (1,)), ((), ())), preferred_element_type=F32
    ) * (1.0 / math.sqrt(HD))
    slot = lax.broadcasted_iota(jnp.int32, scores.shape, 1)
    scores = jnp.where(slot < length, scores, -jnp.inf)
    top = jnp.max(scores, axis=-1, keepdims=True)
    weights = jnp.exp(scores - top)
    total = jnp.sum(weights, axis=-1, keepdims=True)
    out_ref[0, 0] = jnp.dot(weights.astype(BF16), value_ref[0], preferred_element_type=F32)
    top_ref[0, 0] = jnp.broadcast_to(top, top_ref.shape[2:])
    total_ref[0, 0] = jnp.broadcast_to(total, total_ref.shape[2:])


def old_attention(query_heads, cache_keys, cache_values, cache_lengths):
    rows, heads, queries, _ = query_heads.shape
    cache = cache_keys.shape[1]
    small = pl.BlockSpec((1, 1, queries, HD), lambda r, h, lengths: (r, h, 0, 0))
    large = pl.BlockSpec((1, cache, HD), lambda r, h, lengths: (r, 0, h))
    shape = jax.ShapeDtypeStruct((rows, heads, queries, HD), F32)
    return pl.pallas_call(
        old_attention_kernel,
        out_shape=(shape, shape, shape),
        grid_spec=pltpu.PrefetchScalarGridSpec(
            num_scalar_prefetch=1,
            grid=(rows, heads),
            in_specs=[small, large, large],
            out_specs=[small, small, small],
        ),
        compiler_params=pltpu.CompilerParams(vmem_limit_bytes=24 * 1024 * 1024),
        name="old_attention",
    )(cache_lengths, query_heads, cache_keys, cache_values)


def local(
    tokens,
    grad_out,
    weight,
    moment_one,
    moment_two,
    rollout_hidden,
    queries,
    cache_keys,
    cache_values,
    cache_lengths,
    key_gain,
):
    token_count = tokens.shape[0]
    total_tokens = token_count * 64
    own_rows = weight.shape[0]
    columns = weight.shape[1] * weight.shape[2]
    entry_count = own_rows * 64 * columns * 4
    z = lax.axis_index("z")
    xl = lax.axis_index("xl")
    xh = lax.axis_index("xh")
    core = lax.axis_index("core")

    upstream = grad_out.reshape(token_count, columns)
    with jax.named_scope("exchange"):
        tokens_other = swap(tokens, "core")
        upstream_other = swap(upstream, "xh")

    with jax.named_scope("hidden"):
        row_count, step_count, model_width = rollout_hidden.shape
        states = row_count * step_count
        hidden = rollout_hidden.reshape(states, 64, own_rows).transpose(1, 0, 2)
        hidden = lax.all_to_all(hidden, FSDP, 0, 0).reshape(64 * states, own_rows)

    def product(left, right):
        out = lax.dot_general(left, right, (((0,), (0,)), ((), ())), preferred_element_type=F32)
        return out.astype(BF16).reshape(2, 2, 4, own_rows, columns)

    def reduce_xl(block):
        block = block.astype(BF16)
        kept = lax.dynamic_index_in_dim(block, xl, axis=1, keepdims=False)
        sent = lax.dynamic_index_in_dim(block, 1 - xl, axis=1, keepdims=False)
        return (kept.astype(F32) + swap(sent, "xl").astype(F32)).astype(BF16)

    halves = []
    for name, right in (("own", upstream), ("other", upstream_other)):
        with jax.named_scope("gradient_" + name):
            first = reduce_xl(reduce_y(product(tokens, right), 0))
            second = reduce_xl(reduce_y(product(tokens_other, right), 1))
            halves.append(
                jnp.where(
                    core == 0,
                    jnp.concatenate([first, second]),
                    jnp.concatenate([second, first]),
                )
            )
    with jax.named_scope("reduce_z"):
        own, other = halves
        parts = jnp.where(
            xh == 0, jnp.concatenate([own, other]), jnp.concatenate([other, own])
        )
        parts = lax.all_to_all(parts, "z", 0, 0)
        gradient = jnp.sum(parts.astype(F32), axis=0) / total_tokens
    with jax.named_scope("place"):
        pairs = []
        for a in range(8):
            for b in range(2):
                pairs.append((a * 2 + b, a * 2 + b if a // 4 == b else (a + 4) % 8 * 2 + 1 - b))
        placed = lax.ppermute(gradient, ("z", "xh"), pairs)
    with jax.named_scope("squares"):
        squares = jnp.sum(gradient * gradient)
        squares = lax.all_to_all(jnp.broadcast_to(squares, (256, 1, 128)), EVERY, 0, 0)
        squares = jnp.sum(squares[:, 0, 0])
        factor = jnp.minimum(1.0, clip_rms / jnp.sqrt(squares / float(entry_count) + norm_eps))
    with jax.named_scope("adam"):
        new_weight, adam_step = adamw_update(
            weight.reshape(own_rows, columns),
            placed,
            moment_one.reshape(own_rows, columns),
            moment_two.reshape(own_rows, columns),
            factor,
        )
        rollout_weight = new_weight.astype(BF16)
    with jax.named_scope("project"):
        partial = jnp.dot(hidden, rollout_weight, preferred_element_type=F32).astype(BF16)
        partial = lax.all_to_all(partial.reshape(64, states, columns), FSDP, 0, 0)
        projected = jnp.sum(partial.astype(F32), axis=0)

    with jax.named_scope("old"):
        head_count = weight.shape[2] // HD
        groups = QH // KVH
        scale_factor = 1.0 / math.sqrt(HD)
        query_heads = queries.reshape(row_count, step_count, head_count, groups, HD)
        query_heads = query_heads.transpose(0, 2, 1, 3, 4)
        query_heads = query_heads.reshape(row_count, head_count, step_count * groups, HD)
        old_sum, old_top, old_total = old_attention(
            query_heads, cache_keys, cache_values, cache_lengths
        )
    with jax.named_scope("fresh"):
        projected = projected.reshape(row_count, step_count, 2, head_count, HD)
        positions = cache_lengths[:, None] + jnp.arange(step_count, dtype=jnp.int32)[None, :]
        fresh_keys = rotate_keys(
            norm_keys(projected[:, :, 0], key_gain), positions[:, :, None]
        ).astype(BF16)
        fresh_values = projected[:, :, 1].astype(BF16)
        fresh_scores = (
            jnp.einsum("rgqd,rtgd->rgqt", query_heads, fresh_keys, preferred_element_type=F32)
            * scale_factor
        )
        step_of = jnp.arange(step_count * groups) // groups
        fresh_valid = step_of[:, None] >= jnp.arange(step_count)[None, :]
        fresh_scores = jnp.where(fresh_valid, fresh_scores, -jnp.inf)
        old_top = old_top[..., :1]
        old_total = old_total[..., :1]
        top = jnp.maximum(old_top, jnp.max(fresh_scores, axis=-1, keepdims=True))
        fresh_exp = jnp.exp(fresh_scores - top)
        old_scale = jnp.exp(old_top - top)
        denominator = old_total * old_scale + jnp.sum(fresh_exp, axis=-1, keepdims=True)
        mixed = old_sum * (old_scale / denominator)
        mixed = mixed + jnp.einsum(
            "rgqt,rtgd->rgqd",
            (fresh_exp / denominator).astype(BF16),
            fresh_values,
            preferred_element_type=F32,
        )
        attended = mixed.astype(BF16).reshape(row_count, head_count, step_count, groups, HD)
        attended = attended.transpose(0, 2, 1, 3, 4)
        attended = attended.reshape(row_count, step_count, head_count * groups * HD)
        new_keys = fresh_keys.reshape(row_count, step_count, head_count * HD)
        new_values = fresh_values.reshape(row_count, step_count, head_count * HD)
    return (
        new_weight.reshape(weight.shape),
        adam_step.reshape(weight.shape),
        new_keys,
        new_values,
        attended,
    )


def solution(mesh):
    fine = Mesh(mesh.devices.reshape(tuple(SIZES.values())), tuple(SIZES))
    in_specs = (
        P(FSDP, TP),
        P(FSDP, None, TP),
        P(FSDP, None, TP),
        P(FSDP, None, TP),
        P(FSDP, None, TP),
        P(FSDP, None, None),
        P(FSDP, None, TP),
        P(FSDP, None, TP),
        P(FSDP, None, TP),
        P(FSDP),
        P(),
    )
    out_specs = (P(FSDP, None, TP),) * 5
    return jax.shard_map(local, mesh=fine, in_specs=in_specs, out_specs=out_specs, check_vma=False)
```

```python
import functools
import math

import jax
import jax.numpy as jnp
from jax import lax
from jax.experimental import pallas as pl
from jax.experimental.pallas import tpu as pltpu
from jax.sharding import Mesh
from jax.sharding import PartitionSpec as P

QH = 64
KVH = 8
HD = 128

beta_one = 0.9
beta_two = 0.999
learn_rate = 0.001
decay_rate = 0.1
adam_eps = 1e-08
step_number = 10.0
clip_rms = 0.001
norm_eps = 1e-06
rope_base = 1000000.0

SIZES = {"z": 8, "xl": 2, "y": 4, "xh": 2, "core": 2}
FSDP = ("z", "xl", "y")
TP = ("xh", "core")
EVERY = FSDP + TP

BF16 = jnp.bfloat16
F32 = jnp.float32


def adamw_update(weight, gradient, moment_one, moment_two, factor):
    clipped = gradient * factor
    first_moment = beta_one * moment_one + (1.0 - beta_one) * clipped
    second_moment = beta_two * moment_two + (1.0 - beta_two) * clipped * clipped
    first_hat = first_moment / (1.0 - beta_one**step_number)
    second_hat = second_moment / (1.0 - beta_two**step_number)
    direction = first_hat / (jnp.sqrt(second_hat) + adam_eps) + decay_rate * weight
    return (weight - learn_rate * direction, direction)


def swap(values, axis):
    return lax.ppermute(values, axis, [(0, 1), (1, 0)])


PAIRING = ([(0, 1), (1, 0), (2, 3), (3, 2)], [(0, 3), (3, 0), (1, 2), (2, 1)])


def partner(position, pairing):
    return position ^ 1 if pairing == 0 else 3 - position


def in_hbm(values):
    return pltpu.with_memory_space_constraint(values, pltpu.HBM)


def product_kernel(order, left_ref, right_ref, away_ref, near_ref, mine_ref, total_ref):
    total_ref[...] = lax.dot_general(
        left_ref[...], right_ref[...], (((0,), (0,)), ((), ())), preferred_element_type=F32
    )
    rows = mine_ref.shape[2]
    for x in range(2):
        for slot in range(4):
            at = pl.multiple_of((x * 4 + order[slot]) * rows, rows)
            block = total_ref[pl.ds(at, rows), :].astype(BF16)
            if slot < 2:
                away_ref[slot, 0, x] = block
            elif slot == 2:
                near_ref[0, x] = block
            else:
                mine_ref[0, x] = block


def product(left, right, pairing, rows):
    tokens, columns = right.shape
    me = lax.axis_index("y")
    far = partner(me, pairing)
    near = partner(me, 1 - pairing)
    order = jnp.stack([partner(far, 1 - pairing), far, near, me]).astype(jnp.int32)
    part = pltpu.HBM((2, 2, rows, columns), BF16)
    part_spec = pl.BlockSpec((1, 2, rows, columns), lambda k, order: (k, 0, 0, 0))
    return pl.pallas_call(
        product_kernel,
        out_shape=(pltpu.HBM((2, 2, 2, rows, columns), BF16), part, part),
        grid_spec=pltpu.PrefetchScalarGridSpec(
            num_scalar_prefetch=1,
            grid=(2,),
            in_specs=[
                pl.BlockSpec((tokens, 8 * rows), lambda k, order: (0, k)),
                pl.BlockSpec((tokens, columns), lambda k, order: (0, 0)),
            ],
            out_specs=[
                pl.BlockSpec((2, 1, 2, rows, columns), lambda k, order: (0, k, 0, 0, 0)),
                part_spec,
                part_spec,
            ],
            scratch_shapes=[pltpu.VMEM((8 * rows, columns), F32)],
        ),
        compiler_params=pltpu.CompilerParams(vmem_limit_bytes=24 * 1024 * 1024),
        name="product",
    )(order, in_hbm(left), in_hbm(right))


def add(*values):
    total = values[0].astype(F32)
    for value in values[1:]:
        total = total + value.astype(F32)
    return total.astype(BF16)


def along_y(values, pairing):
    return lax.ppermute(values, "y", PAIRING[pairing])


def together(*values):
    return lax.optimization_barrier(values)


def old_attention_kernel(length_ref, query_ref, key_ref, value_ref, out_ref, top_ref, total_ref):
    length = length_ref[pl.program_id(0)]
    scores = lax.dot_general(
        query_ref[0, 0], key_ref[0], (((1,), (1,)), ((), ())), preferred_element_type=F32
    ) * (1.0 / math.sqrt(HD))
    slot = lax.broadcasted_iota(jnp.int32, scores.shape, 1)
    scores = jnp.where(slot < length, scores, -jnp.inf)
    top = jnp.max(scores, axis=-1, keepdims=True)
    weights = jnp.exp(scores - top)
    total = jnp.sum(weights, axis=-1, keepdims=True)
    out_ref[0, 0] = jnp.dot(weights.astype(BF16), value_ref[0], preferred_element_type=F32)
    top_ref[0, 0] = jnp.broadcast_to(top, top_ref.shape[2:])
    total_ref[0, 0] = jnp.broadcast_to(total, total_ref.shape[2:])


def old_attention(query_heads, cache_keys, cache_values, cache_lengths):
    heads, rows, queries, _ = query_heads.shape
    cache = cache_keys.shape[1]
    small = pl.BlockSpec((1, 1, queries, HD), lambda r, h, lengths: (h, r, 0, 0))
    large = pl.BlockSpec((1, cache, HD), lambda r, h, lengths: (r, 0, h))
    shape = jax.ShapeDtypeStruct((heads, rows, queries, HD), F32)
    return pl.pallas_call(
        old_attention_kernel,
        out_shape=(shape, shape, shape),
        grid_spec=pltpu.PrefetchScalarGridSpec(
            num_scalar_prefetch=1,
            grid=(rows, heads),
            in_specs=[small, large, large],
            out_specs=[small, small, small],
        ),
        compiler_params=pltpu.CompilerParams(vmem_limit_bytes=24 * 1024 * 1024),
        name="old_attention",
    )(cache_lengths, query_heads, in_hbm(cache_keys), in_hbm(cache_values))


def fresh_kernel(
    part_ref,
    query_ref,
    old_sum_ref,
    old_top_ref,
    old_total_ref,
    gain_ref,
    cosine_ref,
    sine_ref,
    keys_ref,
    values_ref,
    attended_ref,
    mixed_ref,
    *,
    steps,
):
    heads, queries, _ = query_ref.shape
    states = part_ref.shape[1]
    groups = queries // states
    projected = jnp.sum(part_ref[...].astype(F32), axis=0)
    query = lax.broadcasted_iota(jnp.int32, (queries, states), 0)
    key = lax.broadcasted_iota(jnp.int32, (queries, states), 1)
    row_queries = groups * steps
    valid = (query // row_queries == key // steps) & (query % steps >= key % steps)
    for head in range(heads):
        at = slice(head * HD, (head + 1) * HD)
        raw = projected[:, at]
        mean = jnp.mean(raw * raw, axis=-1, keepdims=True)
        normed = raw * lax.rsqrt(mean + norm_eps) * gain_ref[...]
        turned = normed * cosine_ref[...] + pltpu.roll(normed, HD // 2, 1) * sine_ref[...]
        keys = turned.astype(BF16)
        values = projected[:, heads * HD + head * HD : heads * HD + (head + 1) * HD].astype(BF16)
        keys_ref[:, at] = keys
        values_ref[:, at] = values
        scores = lax.dot_general(
            query_ref[head], keys, (((1,), (1,)), ((), ())), preferred_element_type=F32
        ) * (1.0 / math.sqrt(HD))
        scores = jnp.where(valid, scores, -jnp.inf)
        old_top = old_top_ref[head]
        top = jnp.maximum(old_top, jnp.max(scores, axis=-1, keepdims=True))
        exps = jnp.exp(scores - top[:, :1])
        old_scale = jnp.exp(old_top - top)
        inverse = 1.0 / (old_total_ref[head] * old_scale + jnp.sum(exps, axis=-1, keepdims=True))
        weights = (exps * inverse[:, :1]).astype(BF16)
        mixed = old_sum_ref[head] * (old_scale * inverse)
        mixed = mixed + jnp.dot(weights, values, preferred_element_type=F32)
        for row in range(states // steps):
            for group in range(groups):
                column = (head * groups + group) * HD
                source = row * row_queries + group * steps
                mixed_ref[row * steps : (row + 1) * steps, column : column + HD] = mixed[
                    source : source + steps
                ]
    attended_ref[...] = mixed_ref[...].astype(BF16)


def fresh_attention(parts, query_heads, old_sum, old_top, old_total, key_gain, cosine, sine, steps):
    heads, queries, _ = query_heads.shape
    states = parts.shape[1]
    return pl.pallas_call(
        functools.partial(fresh_kernel, steps=steps),
        out_shape=(
            jax.ShapeDtypeStruct((states, heads * HD), BF16),
            jax.ShapeDtypeStruct((states, heads * HD), BF16),
            jax.ShapeDtypeStruct((states, heads * queries // states * HD), BF16),
        ),
        scratch_shapes=[pltpu.VMEM((states, heads * queries // states * HD), F32)],
        compiler_params=pltpu.CompilerParams(vmem_limit_bytes=24 * 1024 * 1024),
        name="fresh_attention",
    )(parts, query_heads, old_sum, old_top, old_total, key_gain, cosine, sine)


def gradient_kernel(parts_ref, gradient_ref, squares_ref, *, total_tokens):
    gradient = jnp.sum(parts_ref[...].astype(F32), axis=0) / total_tokens
    gradient_ref[...] = gradient
    squares_ref[...] = jnp.broadcast_to(jnp.sum(gradient * gradient), squares_ref.shape)


def sum_gradient(parts, total_tokens, devices):
    return pl.pallas_call(
        functools.partial(gradient_kernel, total_tokens=total_tokens),
        out_shape=(
            jax.ShapeDtypeStruct(parts.shape[1:], F32),
            jax.ShapeDtypeStruct((devices, HD), F32),
        ),
        compiler_params=pltpu.CompilerParams(vmem_limit_bytes=24 * 1024 * 1024),
        name="sum_gradient",
    )(parts)


def update_kernel(
    squares_ref, gradient_ref, state_ref, weight_ref, step_ref, rollout_ref, *, entries
):
    squares = jnp.sum(squares_ref[...], axis=0, keepdims=True)[:, :1]
    factor = jnp.minimum(1.0, clip_rms / jnp.sqrt(squares / entries + norm_eps))
    rows = weight_ref.shape[0]
    new_weight, adam_step = adamw_update(
        state_ref[:rows],
        gradient_ref[...],
        state_ref[rows : 2 * rows],
        state_ref[2 * rows :],
        factor,
    )
    weight_ref[...] = new_weight
    step_ref[...] = adam_step
    rollout_ref[...] = new_weight.astype(BF16)


def update(squares, gradient, state, entries):
    own = jax.ShapeDtypeStruct(gradient.shape, F32)
    return pl.pallas_call(
        functools.partial(update_kernel, entries=entries),
        out_shape=(own, own, jax.ShapeDtypeStruct(gradient.shape, BF16)),
        compiler_params=pltpu.CompilerParams(vmem_limit_bytes=24 * 1024 * 1024),
        name="update",
    )(squares, gradient, state)


def project_kernel(hidden_ref, *refs):
    weights = jnp.concatenate([ref[...] for ref in refs[:-1]])
    partial = jnp.dot(hidden_ref[...], weights, preferred_element_type=F32)
    refs[-1][...] = partial.astype(BF16)


def project(hidden, weights):
    return pl.pallas_call(
        project_kernel,
        out_shape=jax.ShapeDtypeStruct((hidden.shape[0], weights[0].shape[1]), BF16),
        compiler_params=pltpu.CompilerParams(vmem_limit_bytes=24 * 1024 * 1024),
        name="project",
    )(hidden, *weights)


def local(
    tokens,
    grad_out,
    weight,
    moment_one,
    moment_two,
    rollout_hidden,
    queries,
    cache_keys,
    cache_values,
    cache_lengths,
    key_gain,
):
    token_count = tokens.shape[0]
    total_tokens = token_count * 64
    own_rows = weight.shape[0]
    columns = weight.shape[1] * weight.shape[2]
    entry_count = own_rows * 64 * columns * 4
    z = lax.axis_index("z")
    xl = lax.axis_index("xl")
    xh = lax.axis_index("xh")
    core = lax.axis_index("core")

    with jax.named_scope("exchange"):
        upstream_other = swap(grad_out, "xh")
        tokens_other = swap(tokens, "core")
        upstream = grad_out.reshape(token_count, columns)

    row_count, step_count, model_width = rollout_hidden.shape
    states = row_count * step_count
    head_count = weight.shape[2] // HD
    groups = QH // KVH

    def by_xl(first, second):
        block = jnp.stack([first, second])
        kept = lax.dynamic_index_in_dim(block, xl, axis=2, keepdims=False)
        sent = lax.dynamic_index_in_dim(block, 1 - xl, axis=2, keepdims=False)
        return kept, sent

    def in_order(block):
        return jnp.where(core == 0, block, block[::-1]).reshape(4, own_rows, columns)

    def from_y(values, step):
        return lax.ppermute(values, "y", [(a, a ^ step) for a in range(4)])

    with jax.named_scope("first_half"):
        away, one_near, one_mine = product(tokens, upstream, 0, own_rows)
        away, tokens_other, queries, rollout_hidden = together(
            away, tokens_other, queries, rollout_hidden
        )
        one_got = along_y(away, 0)
        away, two_near, two_mine = product(tokens_other, upstream, 1, own_rows)
        two_near, rollout_hidden, weight, moment_one, moment_two = together(
            two_near, rollout_hidden, weight, moment_one, moment_two
        )
        two_got = along_y(away, 1)
    def trade(block, axis, bit, partners):
        mesh_axis = "xl" if bit is None else "z"
        mine = xl if bit is None else (z >> bit) & 1
        kept = lax.dynamic_index_in_dim(block, mine, axis=axis, keepdims=False)
        sent = lax.dynamic_index_in_dim(block, 1 - mine, axis=axis, keepdims=False)
        got = lax.ppermute(sent, mesh_axis, partners)
        return jnp.where(
            mine == 0, jnp.stack([kept, got], axis=axis), jnp.stack([got, kept], axis=axis)
        )

    def trade_z(block, bit):
        return trade(block, 2 - bit, bit, [(a, a ^ (1 << bit)) for a in range(8)])

    with jax.named_scope("hidden"):
        hidden = rollout_hidden.reshape(states, 16, 4 * own_rows).transpose(1, 0, 2)
        hidden = hidden.reshape(2, 2, 2, 2, states, 4 * own_rows)
        hidden = trade(hidden, 3, None, [(0, 1), (1, 0)])
        hidden = trade_z(hidden, 0)
    with jax.named_scope("state"):
        query_heads = queries.reshape(row_count, step_count, head_count, groups, HD)
        query_heads = query_heads.transpose(2, 0, 3, 1, 4)
        query_heads = query_heads.reshape(head_count, row_count, groups * step_count, HD)
        state = jnp.concatenate([weight, moment_one, moment_two]).reshape(3 * own_rows, columns)
    with jax.named_scope("first_half"):
        one_got, two_near, hidden, query_heads, state, upstream_other = together(
            one_got, two_near, hidden, query_heads, state, upstream_other
        )
        one_passed = add(one_near, one_got[0])
        two_passed = add(two_near, two_got[0])
        one_passed, two_passed, upstream_other = together(one_passed, two_passed, upstream_other)
        one_last = along_y(one_passed, 1)
        two_last = along_y(two_passed, 0)
    with jax.named_scope("second_half"):
        upstream_other = upstream_other.reshape(token_count, columns)
        away, three_near, three_mine = product(tokens, upstream_other, 0, own_rows)
        away, tokens_other = together(away, tokens_other)
        three_got = along_y(away, 0)
        away, four_near, four_mine = product(tokens_other, upstream_other, 1, own_rows)
        away, one_last, two_last, hidden = together(away, one_last, two_last, hidden)
        four_got = along_y(away, 1)
    with jax.named_scope("first_half"):
        kept, sent = by_xl(add(one_mine, one_got[1], one_last), add(two_mine, two_got[1], two_last))
        arrived = swap(sent, "xl")
    with jax.named_scope("hidden"):
        hidden = trade_z(trade_z(hidden, 1), 2)
        y = lax.axis_index("y")
        hidden = hidden.reshape(16 * states, 4, own_rows)
        hidden = jnp.concatenate(
            [
                lax.dynamic_index_in_dim(hidden, y ^ step, axis=1, keepdims=False)
                for step in range(4)
            ],
            axis=1,
        )
    with jax.named_scope("second_half"):
        three_got, four_near, hidden = together(three_got, four_near, hidden)
        three_passed = add(three_near, three_got[0])
        four_passed = add(four_near, four_got[0])
        three_passed, four_passed, arrived = together(three_passed, four_passed, arrived)
        three_last = along_y(three_passed, 1)
        four_last = along_y(four_passed, 0)
    with jax.named_scope("first_half"):
        first = in_order(add(kept, arrived))
    with jax.named_scope("second_half"):
        three_last, first = together(three_last, first)
        kept, sent = by_xl(
            add(three_mine, three_got[1], three_last), add(four_mine, four_got[1], four_last)
        )
        second = in_order(add(kept, swap(sent, "xl")))
    with jax.named_scope("reduce_z"):
        parts = jnp.where(
            xh == 0, jnp.concatenate([first, second]), jnp.concatenate([second, first])
        )
        parts = lax.all_to_all(parts, "z", 0, 0)
        gradient, squares = sum_gradient(parts, total_tokens, 256)
    with jax.named_scope("squares"):
        squares = lax.all_to_all(squares, EVERY, 0, 0, tiled=True)
    with jax.named_scope("place"):
        pairs = [(a * 2 + b, (a + 4) % 8 * 2 + 1 - b) for a in range(8) for b in range(2) if a // 4 != b]
        placed = lax.ppermute(gradient, ("z", "xh"), pairs)
        gradient = jnp.where(z // 4 == xh, gradient, placed)
        gradient, squares = together(gradient, squares)
    with jax.named_scope("update"):
        new_weight, adam_step, rollout_weight = update(
            squares, gradient, state, float(entry_count)
        )
    with jax.named_scope("project"):
        weights = [rollout_weight] + [from_y(rollout_weight, step) for step in range(1, 4)]
        partial = project(hidden, weights)
        partial, query_heads = together(partial, query_heads)
        partial = lax.all_to_all(partial.reshape(16, states, columns), ("z", "xl"), 0, 0)
    with jax.named_scope("old"):
        old = old_attention(query_heads, cache_keys, cache_values, cache_lengths)

        def flat(values):
            return values.reshape(head_count, groups * states, HD)

        half_width = HD // 2
        frequency = rope_base ** (-2.0 * jnp.arange(half_width, dtype=F32) / HD)
        positions = cache_lengths[:, None] + jnp.arange(step_count, dtype=jnp.int32)[None, :]
        angles = positions.astype(F32).reshape(states, 1) * frequency
        cosine = jnp.cos(angles)
        sine = jnp.sin(angles)
        cosine = jnp.concatenate([cosine, cosine], axis=-1)
        sine = jnp.concatenate([-sine, sine], axis=-1)
    with jax.named_scope("fresh"):
        new_keys, new_values, attended = fresh_attention(
            partial,
            flat(query_heads),
            *[flat(values) for values in old],
            key_gain.reshape(1, HD),
            cosine,
            sine,
            step_count,
        )
        new_keys = new_keys.reshape(row_count, step_count, head_count * HD)
        new_values = new_values.reshape(row_count, step_count, head_count * HD)
        attended = attended.reshape(row_count, step_count, head_count * groups * HD)
    return (
        new_weight.reshape(own_rows, 2, columns // 2),
        adam_step.reshape(own_rows, 2, columns // 2),
        new_keys,
        new_values,
        attended,
    )


def solution(mesh):
    fine = Mesh(mesh.devices.reshape(tuple(SIZES.values())), tuple(SIZES))
    in_specs = (
        P(FSDP, TP),
        P(FSDP, None, TP),
        P(FSDP, None, TP),
        P(FSDP, None, TP),
        P(FSDP, None, TP),
        P(FSDP, None, None),
        P(FSDP, None, TP),
        P(FSDP, None, TP),
        P(FSDP, None, TP),
        P(FSDP),
        P(),
    )
    out_specs = (P(FSDP, None, TP),) * 5
    return jax.shard_map(local, mesh=fine, in_specs=in_specs, out_specs=out_specs, check_vma=False)
```

```python
import functools
import math

import jax
import jax.numpy as jnp
from jax import lax
from jax.experimental import pallas as pl
from jax.experimental.pallas import tpu as pltpu
from jax.sharding import Mesh
from jax.sharding import PartitionSpec as P

QH = 64
KVH = 8
HD = 128

beta_one = 0.9
beta_two = 0.999
learn_rate = 0.001
decay_rate = 0.1
adam_eps = 1e-08
step_number = 10.0
clip_rms = 0.001
norm_eps = 1e-06
rope_base = 1000000.0

SIZES = {"z": 8, "xl": 2, "y": 4, "xh": 2, "core": 2}
FSDP = ("z", "xl", "y")
TP = ("xh", "core")
EVERY = FSDP + TP

BF16 = jnp.bfloat16
F32 = jnp.float32


def adamw_update(weight, gradient, moment_one, moment_two, factor):
    clipped = gradient * factor
    first_moment = beta_one * moment_one + (1.0 - beta_one) * clipped
    second_moment = beta_two * moment_two + (1.0 - beta_two) * clipped * clipped
    first_hat = first_moment / (1.0 - beta_one**step_number)
    second_hat = second_moment / (1.0 - beta_two**step_number)
    direction = first_hat / (jnp.sqrt(second_hat) + adam_eps) + decay_rate * weight
    return (weight - learn_rate * direction, direction)


def swap(values, axis):
    return lax.ppermute(values, axis, [(0, 1), (1, 0)])


PAIRING = ([(0, 1), (1, 0), (2, 3), (3, 2)], [(0, 3), (3, 0), (1, 2), (2, 1)])


def partner(position, pairing):
    return position ^ 1 if pairing == 0 else 3 - position


def in_hbm(values):
    return pltpu.with_memory_space_constraint(values, pltpu.HBM)


def product_kernel(order, left_ref, right_ref, away_ref, near_ref, mine_ref, total_ref):
    total_ref[...] = lax.dot_general(
        left_ref[...], right_ref[...], (((0,), (0,)), ((), ())), preferred_element_type=F32
    )
    rows = mine_ref.shape[2]
    for x in range(2):
        for slot in range(4):
            at = pl.multiple_of((x * 4 + order[slot]) * rows, rows)
            block = total_ref[pl.ds(at, rows), :].astype(BF16)
            if slot < 2:
                away_ref[slot, x, 0] = block
            elif slot == 2:
                near_ref[x, 0] = block
            else:
                mine_ref[x, 0] = block


def product(left, right, pairing, rows):
    tokens, columns = right.shape
    me = lax.axis_index("y")
    far = partner(me, pairing)
    near = partner(me, 1 - pairing)
    order = jnp.stack([partner(far, 1 - pairing), far, near, me]).astype(jnp.int32)
    part = pltpu.HBM((2, 2, rows, columns), BF16)
    part_spec = pl.BlockSpec((2, 1, rows, columns), lambda k, order: (0, k, 0, 0))
    return pl.pallas_call(
        product_kernel,
        out_shape=(pltpu.HBM((2, 2, 2, rows, columns), BF16), part, part),
        grid_spec=pltpu.PrefetchScalarGridSpec(
            num_scalar_prefetch=1,
            grid=(2,),
            in_specs=[
                pl.BlockSpec((tokens, 8 * rows), lambda k, order: (0, k)),
                pl.BlockSpec((tokens, columns), lambda k, order: (0, 0)),
            ],
            out_specs=[
                pl.BlockSpec((2, 2, 1, rows, columns), lambda k, order: (0, 0, k, 0, 0)),
                part_spec,
                part_spec,
            ],
            scratch_shapes=[pltpu.VMEM((8 * rows, columns), F32)],
        ),
        compiler_params=pltpu.CompilerParams(vmem_limit_bytes=24 * 1024 * 1024),
        name="product",
    )(order, in_hbm(left), in_hbm(right))


def add(*values):
    total = values[0].astype(F32)
    for value in values[1:]:
        total = total + value.astype(F32)
    return total.astype(BF16)


def along_y(values, pairing):
    return lax.ppermute(values, "y", PAIRING[pairing])


def together(*values):
    return lax.optimization_barrier(values)


def old_attention_kernel(length_ref, query_ref, key_ref, value_ref, out_ref, top_ref, total_ref):
    length = length_ref[pl.program_id(0)]
    scores = lax.dot_general(
        query_ref[0, 0], key_ref[0], (((1,), (1,)), ((), ())), preferred_element_type=F32
    ) * (1.0 / math.sqrt(HD))
    slot = lax.broadcasted_iota(jnp.int32, scores.shape, 1)
    scores = jnp.where(slot < length, scores, -jnp.inf)
    top = jnp.max(scores, axis=-1, keepdims=True)
    weights = jnp.exp(scores - top)
    total = jnp.sum(weights, axis=-1, keepdims=True)
    out_ref[0, 0] = jnp.dot(weights.astype(BF16), value_ref[0], preferred_element_type=F32)
    top_ref[0, 0] = jnp.broadcast_to(top, top_ref.shape[2:])
    total_ref[0, 0] = jnp.broadcast_to(total, total_ref.shape[2:])


def old_attention(query_heads, cache_keys, cache_values, cache_lengths):
    heads, rows, queries, _ = query_heads.shape
    cache = cache_keys.shape[1]
    small = pl.BlockSpec((1, 1, queries, HD), lambda r, h, lengths: (h, r, 0, 0))
    large = pl.BlockSpec((1, cache, HD), lambda r, h, lengths: (r, 0, h))
    shape = jax.ShapeDtypeStruct((heads, rows, queries, HD), F32)
    return pl.pallas_call(
        old_attention_kernel,
        out_shape=(shape, shape, shape),
        grid_spec=pltpu.PrefetchScalarGridSpec(
            num_scalar_prefetch=1,
            grid=(rows, heads),
            in_specs=[small, large, large],
            out_specs=[small, small, small],
        ),
        compiler_params=pltpu.CompilerParams(vmem_limit_bytes=24 * 1024 * 1024),
        name="old_attention",
    )(cache_lengths, query_heads, in_hbm(cache_keys), in_hbm(cache_values))


def fresh_kernel(
    part_ref,
    query_ref,
    old_sum_ref,
    old_top_ref,
    old_total_ref,
    gain_ref,
    cosine_ref,
    sine_ref,
    keys_ref,
    values_ref,
    attended_ref,
    mixed_ref,
    *,
    steps,
):
    heads, queries, _ = query_ref.shape
    states = part_ref.shape[1]
    groups = queries // states
    projected = jnp.sum(part_ref[...].astype(F32), axis=0)
    query = lax.broadcasted_iota(jnp.int32, (queries, states), 0)
    key = lax.broadcasted_iota(jnp.int32, (queries, states), 1)
    row_queries = groups * steps
    valid = (query // row_queries == key // steps) & (query % steps >= key % steps)
    for head in range(heads):
        at = slice(head * HD, (head + 1) * HD)
        raw = projected[:, at]
        mean = jnp.mean(raw * raw, axis=-1, keepdims=True)
        normed = raw * lax.rsqrt(mean + norm_eps) * gain_ref[...]
        turned = normed * cosine_ref[...] + pltpu.roll(normed, HD // 2, 1) * sine_ref[...]
        keys = turned.astype(BF16)
        raw_values = projected[:, heads * HD + head * HD : heads * HD + (head + 1) * HD]
        values = raw_values.astype(BF16)
        for row in range(states // steps):
            own = slice(row * steps, (row + 1) * steps)
            keys_ref[row, :, at] = turned[own].astype(BF16)
            values_ref[row, :, at] = raw_values[own].astype(BF16)
        scores = lax.dot_general(
            query_ref[head], keys, (((1,), (1,)), ((), ())), preferred_element_type=F32
        ) * (1.0 / math.sqrt(HD))
        scores = jnp.where(valid, scores, -jnp.inf)
        old_top = old_top_ref[head]
        top = jnp.maximum(old_top, jnp.max(scores, axis=-1, keepdims=True))
        exps = jnp.exp(scores - top[:, :1])
        old_scale = jnp.exp(old_top - top)
        inverse = 1.0 / (old_total_ref[head] * old_scale + jnp.sum(exps, axis=-1, keepdims=True))
        weights = (exps * inverse[:, :1]).astype(BF16)
        mixed = old_sum_ref[head] * (old_scale * inverse)
        mixed = mixed + jnp.dot(weights, values, preferred_element_type=F32)
        for row in range(states // steps):
            for group in range(groups):
                column = (head * groups + group) * HD
                source = row * row_queries + group * steps
                mixed_ref[row * steps : (row + 1) * steps, column : column + HD] = mixed[
                    source : source + steps
                ]
    for row in range(states // steps):
        attended_ref[row] = mixed_ref[row * steps : (row + 1) * steps].astype(BF16)


def fresh_attention(parts, query_heads, old_sum, old_top, old_total, key_gain, cosine, sine, steps):
    heads, queries, _ = query_heads.shape
    states = parts.shape[1]
    return pl.pallas_call(
        functools.partial(fresh_kernel, steps=steps),
        out_shape=(
            jax.ShapeDtypeStruct((states // steps, steps, heads * HD), BF16),
            jax.ShapeDtypeStruct((states // steps, steps, heads * HD), BF16),
            jax.ShapeDtypeStruct((states // steps, steps, heads * queries // states * HD), BF16),
        ),
        scratch_shapes=[pltpu.VMEM((states, heads * queries // states * HD), F32)],
        compiler_params=pltpu.CompilerParams(vmem_limit_bytes=24 * 1024 * 1024),
        name="fresh_attention",
    )(parts, query_heads, old_sum, old_top, old_total, key_gain, cosine, sine)


def gradient_kernel(parts_ref, gradient_ref, squares_ref, *, total_tokens):
    gradient = jnp.sum(parts_ref[...].astype(F32), axis=0) / total_tokens
    gradient_ref[...] = gradient
    squares_ref[...] = jnp.broadcast_to(jnp.sum(gradient * gradient), squares_ref.shape)


def sum_gradient(parts, total_tokens, devices):
    return pl.pallas_call(
        functools.partial(gradient_kernel, total_tokens=total_tokens),
        out_shape=(
            jax.ShapeDtypeStruct(parts.shape[1:], F32),
            jax.ShapeDtypeStruct((devices, HD), F32),
        ),
        compiler_params=pltpu.CompilerParams(vmem_limit_bytes=24 * 1024 * 1024),
        name="sum_gradient",
    )(parts)


def update_kernel(
    squares_ref, gradient_ref, state_ref, weight_ref, step_ref, rollout_ref, *, entries
):
    squares = jnp.sum(squares_ref[...], axis=0, keepdims=True)[:, :1]
    factor = jnp.minimum(1.0, clip_rms / jnp.sqrt(squares / entries + norm_eps))
    rows = weight_ref.shape[0]
    new_weight, adam_step = adamw_update(
        state_ref[:rows],
        gradient_ref[...],
        state_ref[rows : 2 * rows],
        state_ref[2 * rows :],
        factor,
    )
    weight_ref[...] = new_weight
    step_ref[...] = adam_step
    rollout_ref[...] = new_weight.astype(BF16)


def update(squares, gradient, state, entries):
    own = jax.ShapeDtypeStruct(gradient.shape, F32)
    return pl.pallas_call(
        functools.partial(update_kernel, entries=entries),
        out_shape=(own, own, jax.ShapeDtypeStruct(gradient.shape, BF16)),
        compiler_params=pltpu.CompilerParams(vmem_limit_bytes=24 * 1024 * 1024),
        name="update",
    )(squares, gradient, state)


def project_kernel(hidden_ref, *refs):
    weights = jnp.concatenate([ref[...] for ref in refs[:-1]])
    partial = jnp.dot(hidden_ref[...], weights, preferred_element_type=F32)
    refs[-1][...] = partial.astype(BF16)


def project(hidden, weights):
    return pl.pallas_call(
        project_kernel,
        out_shape=jax.ShapeDtypeStruct((hidden.shape[0], weights[0].shape[1]), BF16),
        compiler_params=pltpu.CompilerParams(vmem_limit_bytes=24 * 1024 * 1024),
        name="project",
    )(hidden, *weights)


def local(
    tokens,
    grad_out,
    weight,
    moment_one,
    moment_two,
    rollout_hidden,
    queries,
    cache_keys,
    cache_values,
    cache_lengths,
    key_gain,
):
    token_count = tokens.shape[0]
    total_tokens = token_count * 64
    own_rows = weight.shape[0]
    columns = weight.shape[1] * weight.shape[2]
    entry_count = own_rows * 64 * columns * 4
    z = lax.axis_index("z")
    xl = lax.axis_index("xl")
    xh = lax.axis_index("xh")
    core = lax.axis_index("core")

    with jax.named_scope("exchange"):
        upstream_other = swap(grad_out, "xh")
        tokens_other = swap(tokens, "core")
        upstream = grad_out.reshape(token_count, columns)

    row_count, step_count, model_width = rollout_hidden.shape
    states = row_count * step_count
    head_count = weight.shape[2] // HD
    groups = QH // KVH

    def by_xl(first, second):
        def slots(at):
            return jnp.stack(
                [lax.dynamic_index_in_dim(block, at, keepdims=False) for block in (first, second)]
            )

        return slots(xl), slots(1 - xl)

    def in_order(block):
        return jnp.where(core == 0, block, block[::-1]).reshape(4, own_rows, columns)

    def from_y(values, step):
        return lax.ppermute(values, "y", [(a, a ^ step) for a in range(4)])

    with jax.named_scope("first_half"):
        away, one_near, one_mine = product(tokens, upstream, 0, own_rows)
        away, tokens_other, queries, rollout_hidden = together(
            away, tokens_other, queries, rollout_hidden
        )
        one_got = along_y(away, 0)
        away, two_near, two_mine = product(tokens_other, upstream, 1, own_rows)
        two_near, rollout_hidden, weight, moment_one, moment_two = together(
            two_near, rollout_hidden, weight, moment_one, moment_two
        )
        two_got = along_y(away, 1)
    def trade(block, axis, bit, partners):
        mesh_axis = "xl" if bit is None else "z"
        mine = xl if bit is None else (z >> bit) & 1
        kept = lax.dynamic_index_in_dim(block, mine, axis=axis, keepdims=False)
        sent = lax.dynamic_index_in_dim(block, 1 - mine, axis=axis, keepdims=False)
        got = lax.ppermute(sent, mesh_axis, partners)
        return jnp.where(
            mine == 0, jnp.stack([kept, got], axis=axis), jnp.stack([got, kept], axis=axis)
        )

    def trade_z(block, bit):
        return trade(block, 2 - bit, bit, [(a, a ^ (1 << bit)) for a in range(8)])

    with jax.named_scope("hidden"):
        hidden = rollout_hidden.reshape(states, 16, 4 * own_rows).transpose(1, 0, 2)
        hidden = hidden.reshape(2, 2, 2, 2, states, 4 * own_rows)
        hidden = trade_z(trade_z(hidden, 0), 1)
        hidden, upstream_other = together(hidden, upstream_other)
        hidden = trade_z(hidden, 2)
    with jax.named_scope("state"):
        query_heads = queries.reshape(row_count, step_count, head_count, groups, HD)
        query_heads = query_heads.transpose(2, 0, 3, 1, 4)
        query_heads = query_heads.reshape(head_count, row_count, groups * step_count, HD)
        state = jnp.concatenate([weight, moment_one, moment_two]).reshape(3 * own_rows, columns)
    with jax.named_scope("first_half"):
        upstream_other = upstream_other.reshape(token_count, columns)
        one_got, two_got, hidden, query_heads, state, upstream_other = together(
            one_got, two_got, hidden, query_heads, state, upstream_other
        )
        one_passed = add(one_near, one_got[0])
        one_passed, upstream_other = together(one_passed, upstream_other)
        one_last = along_y(one_passed, 1)
    with jax.named_scope("second_half"):
        away, three_near, three_mine = product(tokens, upstream_other, 0, own_rows)
        away, tokens_other, two_near = together(away, tokens_other, two_near)
        three_got = along_y(away, 0)
    with jax.named_scope("first_half"):
        two_passed = add(two_near, two_got[0])
        two_passed, tokens_other = together(two_passed, tokens_other)
        two_last = along_y(two_passed, 0)
    with jax.named_scope("second_half"):
        away, four_near, four_mine = product(tokens_other, upstream_other, 1, own_rows)
        away, one_last, two_last = together(away, one_last, two_last)
        four_got = along_y(away, 1)
    with jax.named_scope("first_half"):
        kept, sent = by_xl(add(one_mine, one_got[1], one_last), add(two_mine, two_got[1], two_last))
        arrived = swap(sent, "xl")
    with jax.named_scope("second_half"):
        three_passed = add(three_near, three_got[0])
        four_passed = add(four_near, four_got[0])
        three_passed, four_passed, arrived = together(three_passed, four_passed, arrived)
        three_last = along_y(three_passed, 1)
        four_last = along_y(four_passed, 0)
    with jax.named_scope("first_half"):
        first = in_order(add(kept, arrived))
    with jax.named_scope("second_half"):
        three_last, first = together(three_last, first)
        kept, sent = by_xl(
            add(three_mine, three_got[1], three_last), add(four_mine, four_got[1], four_last)
        )
        second = in_order(add(kept, swap(sent, "xl")))
    with jax.named_scope("reduce_z"):
        parts = jnp.where(
            xh == 0, jnp.concatenate([first, second]), jnp.concatenate([second, first])
        )
        parts = lax.all_to_all(parts, "z", 0, 0)
        gradient, squares = sum_gradient(parts, total_tokens, 256)
        gradient, squares, hidden = together(gradient, squares, hidden)
    with jax.named_scope("hidden"):
        hidden = trade(hidden, 3, None, [(0, 1), (1, 0)])
        y = lax.axis_index("y")
        hidden = hidden.reshape(16 * states, 4, own_rows)
        hidden = jnp.concatenate(
            [
                lax.dynamic_index_in_dim(hidden, y ^ step, axis=1, keepdims=False)
                for step in range(4)
            ],
            axis=1,
        )
    with jax.named_scope("squares"):
        squares = lax.all_to_all(squares, EVERY, 0, 0, tiled=True)
    with jax.named_scope("place"):
        pairs = [(a * 2 + b, (a + 4) % 8 * 2 + 1 - b) for a in range(8) for b in range(2) if a // 4 != b]
        placed = lax.ppermute(gradient, ("z", "xh"), pairs)
        gradient = jnp.where(z // 4 == xh, gradient, placed)
        gradient, squares, hidden = together(gradient, squares, hidden)
    with jax.named_scope("update"):
        new_weight, adam_step, rollout_weight = update(
            squares, gradient, state, float(entry_count)
        )
    with jax.named_scope("project"):
        weights = [rollout_weight] + [from_y(rollout_weight, step) for step in range(1, 4)]
        partial = project(hidden, weights)
        partial, query_heads = together(partial, query_heads)
        partial = lax.all_to_all(partial.reshape(16, states, columns), ("z", "xl"), 0, 0)
    with jax.named_scope("old"):
        old = old_attention(query_heads, cache_keys, cache_values, cache_lengths)

        def flat(values):
            return values.reshape(head_count, groups * states, HD)

        half_width = HD // 2
        frequency = rope_base ** (-2.0 * jnp.arange(half_width, dtype=F32) / HD)
        positions = cache_lengths[:, None] + jnp.arange(step_count, dtype=jnp.int32)[None, :]
        angles = positions.astype(F32).reshape(states, 1) * frequency
        cosine = jnp.cos(angles)
        sine = jnp.sin(angles)
        cosine = jnp.concatenate([cosine, cosine], axis=-1)
        sine = jnp.concatenate([-sine, sine], axis=-1)
    with jax.named_scope("fresh"):
        new_keys, new_values, attended = fresh_attention(
            partial,
            flat(query_heads),
            *[flat(values) for values in old],
            key_gain.reshape(1, HD),
            cosine,
            sine,
            step_count,
        )
    return (
        new_weight.reshape(own_rows, 2, columns // 2),
        adam_step.reshape(own_rows, 2, columns // 2),
        new_keys,
        new_values,
        attended,
    )


def solution(mesh):
    fine = Mesh(mesh.devices.reshape(tuple(SIZES.values())), tuple(SIZES))
    in_specs = (
        P(FSDP, TP),
        P(FSDP, None, TP),
        P(FSDP, None, TP),
        P(FSDP, None, TP),
        P(FSDP, None, TP),
        P(FSDP, None, None),
        P(FSDP, None, TP),
        P(FSDP, None, TP),
        P(FSDP, None, TP),
        P(FSDP),
        P(),
    )
    out_specs = (P(FSDP, None, TP),) * 5
    return jax.shard_map(local, mesh=fine, in_specs=in_specs, out_specs=out_specs, check_vma=False)
```

```python
import functools
import math

import jax
import jax.numpy as jnp
from jax import lax
from jax.experimental import pallas as pl
from jax.experimental.pallas import tpu as pltpu
from jax.sharding import Mesh
from jax.sharding import PartitionSpec as P

QH = 64
KVH = 8
HD = 128

beta_one = 0.9
beta_two = 0.999
learn_rate = 0.001
decay_rate = 0.1
adam_eps = 1e-08
step_number = 10.0
clip_rms = 0.001
norm_eps = 1e-06
rope_base = 1000000.0

SIZES = {"z": 8, "xl": 2, "y": 4, "xh": 2, "core": 2}
FSDP = ("z", "xl", "y")
TP = ("xh", "core")
EVERY = FSDP + TP

BF16 = jnp.bfloat16
F32 = jnp.float32


def adamw_update(weight, gradient, moment_one, moment_two, factor):
    clipped = gradient * factor
    first_moment = beta_one * moment_one + (1.0 - beta_one) * clipped
    second_moment = beta_two * moment_two + (1.0 - beta_two) * clipped * clipped
    first_hat = first_moment / (1.0 - beta_one**step_number)
    second_hat = second_moment / (1.0 - beta_two**step_number)
    direction = first_hat / (jnp.sqrt(second_hat) + adam_eps) + decay_rate * weight
    return (weight - learn_rate * direction, direction)


def swap(values, axis):
    return lax.ppermute(values, axis, [(0, 1), (1, 0)])


PAIRING = ([(0, 1), (1, 0), (2, 3), (3, 2)], [(0, 3), (3, 0), (1, 2), (2, 1)])


def partner(position, pairing):
    return position ^ 1 if pairing == 0 else 3 - position


def in_hbm(values):
    return pltpu.with_memory_space_constraint(values, pltpu.HBM)


def product_kernel(order, left_ref, right_ref, away_ref, near_ref, mine_ref, total_ref):
    total_ref[...] = lax.dot_general(
        left_ref[...], right_ref[...], (((0,), (0,)), ((), ())), preferred_element_type=F32
    )
    rows = mine_ref.shape[2]
    for x in range(2):
        for slot in range(4):
            at = pl.multiple_of((x * 4 + order[slot]) * rows, rows)
            block = total_ref[pl.ds(at, rows), :].astype(BF16)
            if slot < 2:
                away_ref[slot, x, 0] = block
            elif slot == 2:
                near_ref[x, 0] = block
            else:
                mine_ref[x, 0] = block


def product(left, right, pairing, rows):
    tokens, columns = right.shape
    me = lax.axis_index("y")
    far = partner(me, pairing)
    near = partner(me, 1 - pairing)
    order = jnp.stack([partner(far, 1 - pairing), far, near, me]).astype(jnp.int32)
    part = pltpu.HBM((2, 2, rows, columns), BF16)
    part_spec = pl.BlockSpec((2, 1, rows, columns), lambda k, order: (0, k, 0, 0))
    return pl.pallas_call(
        product_kernel,
        out_shape=(pltpu.HBM((2, 2, 2, rows, columns), BF16), part, part),
        grid_spec=pltpu.PrefetchScalarGridSpec(
            num_scalar_prefetch=1,
            grid=(2,),
            in_specs=[
                pl.BlockSpec((tokens, 8 * rows), lambda k, order: (0, k)),
                pl.BlockSpec((tokens, columns), lambda k, order: (0, 0)),
            ],
            out_specs=[
                pl.BlockSpec((2, 2, 1, rows, columns), lambda k, order: (0, 0, k, 0, 0)),
                part_spec,
                part_spec,
            ],
            scratch_shapes=[pltpu.VMEM((8 * rows, columns), F32)],
        ),
        compiler_params=pltpu.CompilerParams(vmem_limit_bytes=24 * 1024 * 1024),
        name="product",
    )(order, in_hbm(left), in_hbm(right))


def add(*values):
    total = values[0].astype(F32)
    for value in values[1:]:
        total = total + value.astype(F32)
    return total.astype(BF16)


def along_y(values, pairing):
    return lax.ppermute(values, "y", PAIRING[pairing])


def together(*values):
    return lax.optimization_barrier(values)


def old_attention_kernel(length_ref, query_ref, key_ref, value_ref, out_ref, top_ref, total_ref):
    length = length_ref[pl.program_id(0)]
    scores = lax.dot_general(
        query_ref[0, 0], key_ref[0], (((1,), (1,)), ((), ())), preferred_element_type=F32
    ) * (1.0 / math.sqrt(HD))
    slot = lax.broadcasted_iota(jnp.int32, scores.shape, 1)
    scores = jnp.where(slot < length, scores, -jnp.inf)
    top = jnp.max(scores, axis=-1, keepdims=True)
    weights = jnp.exp(scores - top)
    total = jnp.sum(weights, axis=-1, keepdims=True)
    out_ref[0, 0] = jnp.dot(weights.astype(BF16), value_ref[0], preferred_element_type=F32)
    top_ref[0, 0] = jnp.broadcast_to(top, top_ref.shape[2:])
    total_ref[0, 0] = jnp.broadcast_to(total, total_ref.shape[2:])


def old_attention(query_heads, cache_keys, cache_values, cache_lengths):
    heads, rows, queries, _ = query_heads.shape
    cache = cache_keys.shape[1]
    small = pl.BlockSpec((1, 1, queries, HD), lambda r, h, lengths: (h, r, 0, 0))
    large = pl.BlockSpec((1, cache, HD), lambda r, h, lengths: (r, 0, h))
    shape = jax.ShapeDtypeStruct((heads, rows, queries, HD), F32)
    return pl.pallas_call(
        old_attention_kernel,
        out_shape=(shape, shape, shape),
        grid_spec=pltpu.PrefetchScalarGridSpec(
            num_scalar_prefetch=1,
            grid=(rows, heads),
            in_specs=[small, large, large],
            out_specs=[small, small, small],
        ),
        compiler_params=pltpu.CompilerParams(vmem_limit_bytes=24 * 1024 * 1024),
        name="old_attention",
    )(cache_lengths, query_heads, in_hbm(cache_keys), in_hbm(cache_values))


def fresh_kernel(
    part_ref,
    query_ref,
    old_sum_ref,
    old_top_ref,
    old_total_ref,
    gain_ref,
    cosine_ref,
    sine_ref,
    keys_ref,
    values_ref,
    attended_ref,
    mixed_ref,
    *,
    steps,
):
    heads, queries, _ = query_ref.shape
    states = part_ref.shape[1]
    groups = queries // states
    projected = jnp.sum(part_ref[...].astype(F32), axis=0)
    query = lax.broadcasted_iota(jnp.int32, (queries, states), 0)
    key = lax.broadcasted_iota(jnp.int32, (queries, states), 1)
    row_queries = groups * steps
    valid = (query // row_queries == key // steps) & (query % steps >= key % steps)
    for head in range(heads):
        at = slice(head * HD, (head + 1) * HD)
        raw = projected[:, at]
        mean = jnp.mean(raw * raw, axis=-1, keepdims=True)
        normed = raw * lax.rsqrt(mean + norm_eps) * gain_ref[...]
        turned = normed * cosine_ref[...] + pltpu.roll(normed, HD // 2, 1) * sine_ref[...]
        keys = turned.astype(BF16)
        raw_values = projected[:, heads * HD + head * HD : heads * HD + (head + 1) * HD]
        values = raw_values.astype(BF16)
        for row in range(states // steps):
            own = slice(row * steps, (row + 1) * steps)
            keys_ref[row, :, at] = turned[own].astype(BF16)
            values_ref[row, :, at] = raw_values[own].astype(BF16)
        scores = lax.dot_general(
            query_ref[head], keys, (((1,), (1,)), ((), ())), preferred_element_type=F32
        ) * (1.0 / math.sqrt(HD))
        scores = jnp.where(valid, scores, -jnp.inf)
        old_top = old_top_ref[head]
        top = jnp.maximum(old_top, jnp.max(scores, axis=-1, keepdims=True))
        exps = jnp.exp(scores - top[:, :1])
        old_scale = jnp.exp(old_top - top)
        inverse = 1.0 / (old_total_ref[head] * old_scale + jnp.sum(exps, axis=-1, keepdims=True))
        weights = (exps * inverse[:, :1]).astype(BF16)
        mixed = old_sum_ref[head] * (old_scale * inverse)
        mixed = mixed + jnp.dot(weights, values, preferred_element_type=F32)
        for row in range(states // steps):
            for group in range(groups):
                column = (head * groups + group) * HD
                source = row * row_queries + group * steps
                mixed_ref[row * steps : (row + 1) * steps, column : column + HD] = mixed[
                    source : source + steps
                ]
    for row in range(states // steps):
        attended_ref[row] = mixed_ref[row * steps : (row + 1) * steps].astype(BF16)


def fresh_attention(parts, query_heads, old_sum, old_top, old_total, key_gain, cosine, sine, steps):
    heads, queries, _ = query_heads.shape
    states = parts.shape[1]
    return pl.pallas_call(
        functools.partial(fresh_kernel, steps=steps),
        out_shape=(
            jax.ShapeDtypeStruct((states // steps, steps, heads * HD), BF16),
            jax.ShapeDtypeStruct((states // steps, steps, heads * HD), BF16),
            jax.ShapeDtypeStruct((states // steps, steps, heads * queries // states * HD), BF16),
        ),
        scratch_shapes=[pltpu.VMEM((states, heads * queries // states * HD), F32)],
        compiler_params=pltpu.CompilerParams(vmem_limit_bytes=24 * 1024 * 1024),
        name="fresh_attention",
    )(parts, query_heads, old_sum, old_top, old_total, key_gain, cosine, sine)


def gradient_kernel(parts_ref, gradient_ref, squares_ref, *, total_tokens):
    gradient = jnp.sum(parts_ref[...].astype(F32), axis=0) / total_tokens
    gradient_ref[...] = gradient
    squares_ref[...] = jnp.broadcast_to(jnp.sum(gradient * gradient), squares_ref.shape)


def sum_gradient(parts, total_tokens, devices):
    return pl.pallas_call(
        functools.partial(gradient_kernel, total_tokens=total_tokens),
        out_shape=(
            jax.ShapeDtypeStruct(parts.shape[1:], F32),
            jax.ShapeDtypeStruct((devices, HD), F32),
        ),
        compiler_params=pltpu.CompilerParams(vmem_limit_bytes=24 * 1024 * 1024),
        name="sum_gradient",
    )(parts)


def update_kernel(
    squares_ref, gradient_ref, state_ref, weight_ref, step_ref, rollout_ref, *, entries
):
    squares = jnp.sum(squares_ref[...], axis=0, keepdims=True)[:, :1]
    factor = jnp.minimum(1.0, clip_rms / jnp.sqrt(squares / entries + norm_eps))
    rows = weight_ref.shape[0]
    new_weight, adam_step = adamw_update(
        state_ref[:rows],
        gradient_ref[...],
        state_ref[rows : 2 * rows],
        state_ref[2 * rows :],
        factor,
    )
    weight_ref[...] = new_weight
    step_ref[...] = adam_step
    rollout_ref[...] = new_weight.astype(BF16)


def update(squares, gradient, state, entries):
    own = jax.ShapeDtypeStruct(gradient.shape, F32)
    return pl.pallas_call(
        functools.partial(update_kernel, entries=entries),
        out_shape=(own, own, jax.ShapeDtypeStruct(gradient.shape, BF16)),
        compiler_params=pltpu.CompilerParams(vmem_limit_bytes=24 * 1024 * 1024),
        name="update",
    )(squares, gradient, state)


def project_kernel(hidden_ref, *refs):
    weights = jnp.concatenate([ref[...] for ref in refs[:-1]])
    partial = jnp.dot(hidden_ref[...], weights, preferred_element_type=F32)
    refs[-1][...] = partial.astype(BF16)


def project(hidden, weights):
    return pl.pallas_call(
        project_kernel,
        out_shape=jax.ShapeDtypeStruct((hidden.shape[0], weights[0].shape[1]), BF16),
        compiler_params=pltpu.CompilerParams(vmem_limit_bytes=24 * 1024 * 1024),
        name="project",
    )(hidden, *weights)


def local(
    tokens,
    grad_out,
    weight,
    moment_one,
    moment_two,
    rollout_hidden,
    queries,
    cache_keys,
    cache_values,
    cache_lengths,
    key_gain,
):
    token_count = tokens.shape[0]
    total_tokens = token_count * 64
    own_rows = weight.shape[0]
    columns = weight.shape[1] * weight.shape[2]
    entry_count = own_rows * 64 * columns * 4
    z = lax.axis_index("z")
    xl = lax.axis_index("xl")
    xh = lax.axis_index("xh")
    core = lax.axis_index("core")

    with jax.named_scope("exchange"):
        upstream_other = swap(grad_out, "xh")
        tokens_other = swap(tokens, "core")
        upstream = grad_out.reshape(token_count, columns)

    row_count, step_count, model_width = rollout_hidden.shape
    states = row_count * step_count
    head_count = weight.shape[2] // HD
    groups = QH // KVH

    def by_xl(first, second):
        def slots(at):
            return jnp.stack(
                [lax.dynamic_index_in_dim(block, at, keepdims=False) for block in (first, second)]
            )

        return slots(xl), slots(1 - xl)

    def in_order(block):
        return jnp.where(core == 0, block, block[::-1]).reshape(4, own_rows, columns)

    def from_y(values, step):
        return lax.ppermute(values, "y", [(a, a ^ step) for a in range(4)])

    def trade(block, axis, bit, partners):
        mesh_axis = "xl" if bit is None else "z"
        mine = xl if bit is None else (z >> bit) & 1
        kept = lax.dynamic_index_in_dim(block, mine, axis=axis, keepdims=False)
        sent = lax.dynamic_index_in_dim(block, 1 - mine, axis=axis, keepdims=False)
        got = lax.ppermute(sent, mesh_axis, partners)
        return jnp.where(
            mine == 0, jnp.stack([kept, got], axis=axis), jnp.stack([got, kept], axis=axis)
        )

    def trade_z(block, bit):
        return trade(block, 2 - bit, bit, [(a, a ^ (1 << bit)) for a in range(8)])

    with jax.named_scope("first_half"):
        away, one_near, one_mine = product(tokens, upstream, 0, own_rows)
        away, tokens_other, queries, rollout_hidden = together(
            away, tokens_other, queries, rollout_hidden
        )
        one_got = along_y(away, 0)
    with jax.named_scope("hidden"):
        hidden = rollout_hidden.reshape(states, 16, 4 * own_rows).transpose(1, 0, 2)
        hidden = hidden.reshape(2, 2, 2, 2, states, 4 * own_rows)
        hidden = trade_z(hidden, 0)
    with jax.named_scope("first_half"):
        away, two_near, two_mine = product(tokens_other, upstream, 1, own_rows)
        two_near, hidden, weight, moment_one, moment_two = together(
            two_near, hidden, weight, moment_one, moment_two
        )
        two_got = along_y(away, 1)
    with jax.named_scope("hidden"):
        hidden = trade_z(trade_z(hidden, 1), 2)
        hidden, upstream_other = together(hidden, upstream_other)
    with jax.named_scope("state"):
        query_heads = queries.reshape(row_count, step_count, head_count, groups, HD)
        query_heads = query_heads.transpose(2, 0, 3, 1, 4)
        query_heads = query_heads.reshape(head_count, row_count, groups * step_count, HD)
        state = jnp.concatenate([weight, moment_one, moment_two]).reshape(3 * own_rows, columns)
    with jax.named_scope("first_half"):
        upstream_other = upstream_other.reshape(token_count, columns)
        one_got, two_got, hidden, query_heads, state, upstream_other = together(
            one_got, two_got, hidden, query_heads, state, upstream_other
        )
        one_passed = add(one_near, one_got[0])
        one_passed, upstream_other = together(one_passed, upstream_other)
        one_last = along_y(one_passed, 1)
    with jax.named_scope("second_half"):
        away, three_near, three_mine = product(tokens, upstream_other, 0, own_rows)
        away, tokens_other, two_near = together(away, tokens_other, two_near)
        three_got = along_y(away, 0)
    with jax.named_scope("first_half"):
        two_passed = add(two_near, two_got[0])
        two_passed, tokens_other = together(two_passed, tokens_other)
        two_last = along_y(two_passed, 0)
    with jax.named_scope("second_half"):
        away, four_near, four_mine = product(tokens_other, upstream_other, 1, own_rows)
        away, one_last, two_last = together(away, one_last, two_last)
        four_got = along_y(away, 1)
    with jax.named_scope("first_half"):
        kept, sent = by_xl(add(one_mine, one_got[1], one_last), add(two_mine, two_got[1], two_last))
        sent, query_heads = together(sent, query_heads)
        arrived = swap(sent, "xl")
    with jax.named_scope("old"):
        old = old_attention(query_heads, cache_keys, cache_values, cache_lengths)
        three_got, *old = together(three_got, *old)
    with jax.named_scope("second_half"):
        three_passed = add(three_near, three_got[0])
        four_passed = add(four_near, four_got[0])
        three_passed, four_passed, arrived = together(three_passed, four_passed, arrived)
        three_last = along_y(three_passed, 1)
        four_last = along_y(four_passed, 0)
    with jax.named_scope("first_half"):
        first = in_order(add(kept, arrived))
    with jax.named_scope("second_half"):
        three_last, first = together(three_last, first)
        kept, sent = by_xl(
            add(three_mine, three_got[1], three_last), add(four_mine, four_got[1], four_last)
        )
        second = in_order(add(kept, swap(sent, "xl")))
    with jax.named_scope("reduce_z"):
        parts = jnp.where(
            xh == 0, jnp.concatenate([first, second]), jnp.concatenate([second, first])
        )
        parts = lax.all_to_all(parts, "z", 0, 0)
        gradient, squares = sum_gradient(parts, total_tokens, 256)
        gradient, squares, hidden = together(gradient, squares, hidden)
    with jax.named_scope("hidden"):
        hidden = trade(hidden, 3, None, [(0, 1), (1, 0)])
        y = lax.axis_index("y")
        hidden = hidden.reshape(16 * states, 4, own_rows)
        hidden = jnp.concatenate(
            [
                lax.dynamic_index_in_dim(hidden, y ^ step, axis=1, keepdims=False)
                for step in range(4)
            ],
            axis=1,
        )
    with jax.named_scope("squares"):
        squares = lax.all_to_all(squares, EVERY, 0, 0, tiled=True)
    with jax.named_scope("place"):
        pairs = [(a * 2 + b, (a + 4) % 8 * 2 + 1 - b) for a in range(8) for b in range(2) if a // 4 != b]
        placed = lax.ppermute(gradient, ("z", "xh"), pairs)
        gradient = jnp.where(z // 4 == xh, gradient, placed)
        gradient, squares, hidden = together(gradient, squares, hidden)
    with jax.named_scope("update"):
        new_weight, adam_step, rollout_weight = update(
            squares, gradient, state, float(entry_count)
        )
    with jax.named_scope("project"):
        weights = [rollout_weight] + [from_y(rollout_weight, step) for step in range(1, 4)]
        partial = project(hidden, weights)
        partial = lax.all_to_all(partial.reshape(16, states, columns), ("z", "xl"), 0, 0)
    with jax.named_scope("angles"):
        half_width = HD // 2
        frequency = rope_base ** (-2.0 * jnp.arange(half_width, dtype=F32) / HD)
        positions = cache_lengths[:, None] + jnp.arange(step_count, dtype=jnp.int32)[None, :]
        angles = positions.astype(F32).reshape(states, 1) * frequency
        cosine = jnp.cos(angles)
        sine = jnp.sin(angles)
        cosine = jnp.concatenate([cosine, cosine], axis=-1)
        sine = jnp.concatenate([-sine, sine], axis=-1)
    with jax.named_scope("fresh"):
        new_keys, new_values, attended = fresh_attention(
            partial,
            *[
                values.reshape(head_count, groups * states, HD)
                for values in (query_heads, *old)
            ],
            key_gain.reshape(1, HD),
            cosine,
            sine,
            step_count,
        )
    return (
        new_weight.reshape(own_rows, 2, columns // 2),
        adam_step.reshape(own_rows, 2, columns // 2),
        new_keys,
        new_values,
        attended,
    )


def solution(mesh):
    fine = Mesh(mesh.devices.reshape(tuple(SIZES.values())), tuple(SIZES))
    in_specs = (
        P(FSDP, TP),
        P(FSDP, None, TP),
        P(FSDP, None, TP),
        P(FSDP, None, TP),
        P(FSDP, None, TP),
        P(FSDP, None, None),
        P(FSDP, None, TP),
        P(FSDP, None, TP),
        P(FSDP, None, TP),
        P(FSDP),
        P(),
    )
    out_specs = (P(FSDP, None, TP),) * 5
    return jax.shard_map(local, mesh=fine, in_specs=in_specs, out_specs=out_specs, check_vma=False)
```

```python
import functools
import math

import jax
import jax.numpy as jnp
from jax import lax
from jax.experimental import pallas as pl
from jax.experimental.pallas import tpu as pltpu
from jax.sharding import Mesh
from jax.sharding import PartitionSpec as P

QH = 64
KVH = 8
HD = 128

beta_one = 0.9
beta_two = 0.999
learn_rate = 0.001
decay_rate = 0.1
adam_eps = 1e-08
step_number = 10.0
clip_rms = 0.001
norm_eps = 1e-06
rope_base = 1000000.0

SIZES = {"z": 8, "xl": 2, "y": 4, "xh": 2, "core": 2}
FSDP = ("z", "xl", "y")
TP = ("xh", "core")
EVERY = FSDP + TP

BF16 = jnp.bfloat16
F32 = jnp.float32


def adamw_update(weight, gradient, moment_one, moment_two, factor):
    clipped = gradient * factor
    first_moment = beta_one * moment_one + (1.0 - beta_one) * clipped
    second_moment = beta_two * moment_two + (1.0 - beta_two) * clipped * clipped
    first_hat = first_moment / (1.0 - beta_one**step_number)
    second_hat = second_moment / (1.0 - beta_two**step_number)
    direction = first_hat / (jnp.sqrt(second_hat) + adam_eps) + decay_rate * weight
    return (weight - learn_rate * direction, direction)


def swap(values, axis):
    return lax.ppermute(values, axis, [(0, 1), (1, 0)])


PAIRING = ([(0, 1), (1, 0), (2, 3), (3, 2)], [(0, 3), (3, 0), (1, 2), (2, 1)])


def partner(position, pairing):
    return position ^ 1 if pairing == 0 else 3 - position


def in_hbm(values):
    return pltpu.with_memory_space_constraint(values, pltpu.HBM)


def product_kernel(order, left_ref, right_ref, away_ref, near_ref, mine_ref, total_ref):
    total_ref[...] = lax.dot_general(
        left_ref[...], right_ref[...], (((0,), (0,)), ((), ())), preferred_element_type=F32
    )
    rows = mine_ref.shape[2]
    for x in range(2):
        for slot in range(4):
            at = pl.multiple_of((x * 4 + order[slot]) * rows, rows)
            block = total_ref[pl.ds(at, rows), :].astype(BF16)
            if slot < 2:
                away_ref[slot, x, 0] = block
            elif slot == 2:
                near_ref[x, 0] = block
            else:
                mine_ref[x, 0] = block


def product(left, right, pairing, rows):
    tokens, columns = right.shape
    me = lax.axis_index("y")
    far = partner(me, pairing)
    near = partner(me, 1 - pairing)
    order = jnp.stack([partner(far, 1 - pairing), far, near, me]).astype(jnp.int32)
    part = pltpu.HBM((2, 2, rows, columns), BF16)
    part_spec = pl.BlockSpec((2, 1, rows, columns), lambda k, order: (0, k, 0, 0))
    return pl.pallas_call(
        product_kernel,
        out_shape=(pltpu.HBM((2, 2, 2, rows, columns), BF16), part, part),
        grid_spec=pltpu.PrefetchScalarGridSpec(
            num_scalar_prefetch=1,
            grid=(2,),
            in_specs=[
                pl.BlockSpec((tokens, 8 * rows), lambda k, order: (0, k)),
                pl.BlockSpec((tokens, columns), lambda k, order: (0, 0)),
            ],
            out_specs=[
                pl.BlockSpec((2, 2, 1, rows, columns), lambda k, order: (0, 0, k, 0, 0)),
                part_spec,
                part_spec,
            ],
            scratch_shapes=[pltpu.VMEM((8 * rows, columns), F32)],
        ),
        compiler_params=pltpu.CompilerParams(vmem_limit_bytes=24 * 1024 * 1024),
        name="product",
    )(order, in_hbm(left), right)


def add(*values):
    total = values[0].astype(F32)
    for value in values[1:]:
        total = total + value.astype(F32)
    return total.astype(BF16)


def along_y(values, pairing):
    return lax.ppermute(values, "y", PAIRING[pairing])


def together(*values):
    return lax.optimization_barrier(values)


def old_attention_kernel(length_ref, query_ref, key_ref, value_ref, out_ref, top_ref, total_ref):
    length = length_ref[pl.program_id(0)]
    scores = lax.dot_general(
        query_ref[0, 0], key_ref[0], (((1,), (1,)), ((), ())), preferred_element_type=F32
    ) * (1.0 / math.sqrt(HD))
    slot = lax.broadcasted_iota(jnp.int32, scores.shape, 1)
    scores = jnp.where(slot < length, scores, -jnp.inf)
    top = jnp.max(scores, axis=-1, keepdims=True)
    weights = jnp.exp(scores - top)
    total = jnp.sum(weights, axis=-1, keepdims=True)
    out_ref[0, 0] = jnp.dot(weights.astype(BF16), value_ref[0], preferred_element_type=F32)
    top_ref[0, 0] = jnp.broadcast_to(top, top_ref.shape[2:])
    total_ref[0, 0] = jnp.broadcast_to(total, total_ref.shape[2:])


def old_attention(query_heads, cache_keys, cache_values, cache_lengths):
    heads, rows, queries, _ = query_heads.shape
    cache = cache_keys.shape[1]
    small = pl.BlockSpec((1, 1, queries, HD), lambda r, h, lengths: (h, r, 0, 0))
    large = pl.BlockSpec((1, cache, HD), lambda r, h, lengths: (r, 0, h))
    shape = jax.ShapeDtypeStruct((heads, rows, queries, HD), F32)
    return pl.pallas_call(
        old_attention_kernel,
        out_shape=(shape, shape, shape),
        grid_spec=pltpu.PrefetchScalarGridSpec(
            num_scalar_prefetch=1,
            grid=(rows, heads),
            in_specs=[small, large, large],
            out_specs=[small, small, small],
        ),
        compiler_params=pltpu.CompilerParams(vmem_limit_bytes=24 * 1024 * 1024),
        name="old_attention",
    )(cache_lengths, query_heads, in_hbm(cache_keys), in_hbm(cache_values))


def fresh_kernel(
    part_ref,
    query_ref,
    old_sum_ref,
    old_top_ref,
    old_total_ref,
    gain_ref,
    cosine_ref,
    sine_ref,
    keys_ref,
    values_ref,
    attended_ref,
    mixed_ref,
    *,
    steps,
):
    heads, queries, _ = query_ref.shape
    states = part_ref.shape[1]
    groups = queries // states
    projected = jnp.sum(part_ref[...].astype(F32), axis=0)
    query = lax.broadcasted_iota(jnp.int32, (queries, states), 0)
    key = lax.broadcasted_iota(jnp.int32, (queries, states), 1)
    row_queries = groups * steps
    valid = (query // row_queries == key // steps) & (query % steps >= key % steps)
    for head in range(heads):
        at = slice(head * HD, (head + 1) * HD)
        raw = projected[:, at]
        mean = jnp.mean(raw * raw, axis=-1, keepdims=True)
        normed = raw * lax.rsqrt(mean + norm_eps) * gain_ref[...]
        turned = normed * cosine_ref[...] + pltpu.roll(normed, HD // 2, 1) * sine_ref[...]
        keys = turned.astype(BF16)
        raw_values = projected[:, heads * HD + head * HD : heads * HD + (head + 1) * HD]
        values = raw_values.astype(BF16)
        for row in range(states // steps):
            own = slice(row * steps, (row + 1) * steps)
            keys_ref[row, :, at] = turned[own].astype(BF16)
            values_ref[row, :, at] = raw_values[own].astype(BF16)
        scores = lax.dot_general(
            query_ref[head], keys, (((1,), (1,)), ((), ())), preferred_element_type=F32
        ) * (1.0 / math.sqrt(HD))
        scores = jnp.where(valid, scores, -jnp.inf)
        old_top = old_top_ref[head]
        top = jnp.maximum(old_top, jnp.max(scores, axis=-1, keepdims=True))
        exps = jnp.exp(scores - top[:, :1])
        old_scale = jnp.exp(old_top - top)
        inverse = 1.0 / (old_total_ref[head] * old_scale + jnp.sum(exps, axis=-1, keepdims=True))
        weights = (exps * inverse[:, :1]).astype(BF16)
        mixed = old_sum_ref[head] * (old_scale * inverse)
        mixed = mixed + jnp.dot(weights, values, preferred_element_type=F32)
        for row in range(states // steps):
            for group in range(groups):
                column = (head * groups + group) * HD
                source = row * row_queries + group * steps
                mixed_ref[row * steps : (row + 1) * steps, column : column + HD] = mixed[
                    source : source + steps
                ]
    for row in range(states // steps):
        attended_ref[row] = mixed_ref[row * steps : (row + 1) * steps].astype(BF16)


def fresh_attention(parts, query_heads, old_sum, old_top, old_total, key_gain, cosine, sine, steps):
    heads, queries, _ = query_heads.shape
    states = parts.shape[1]
    return pl.pallas_call(
        functools.partial(fresh_kernel, steps=steps),
        out_shape=(
            jax.ShapeDtypeStruct((states // steps, steps, heads * HD), BF16),
            jax.ShapeDtypeStruct((states // steps, steps, heads * HD), BF16),
            jax.ShapeDtypeStruct((states // steps, steps, heads * queries // states * HD), BF16),
        ),
        scratch_shapes=[pltpu.VMEM((states, heads * queries // states * HD), F32)],
        compiler_params=pltpu.CompilerParams(vmem_limit_bytes=24 * 1024 * 1024),
        name="fresh_attention",
    )(parts, query_heads, old_sum, old_top, old_total, key_gain, cosine, sine)


def gradient_kernel(parts_ref, gradient_ref, squares_ref, *, total_tokens):
    gradient = jnp.sum(parts_ref[...].astype(F32), axis=0) / total_tokens
    gradient_ref[...] = gradient
    squares_ref[...] = jnp.broadcast_to(jnp.sum(gradient * gradient), squares_ref.shape)


def sum_gradient(parts, total_tokens, devices):
    return pl.pallas_call(
        functools.partial(gradient_kernel, total_tokens=total_tokens),
        out_shape=(
            jax.ShapeDtypeStruct(parts.shape[1:], F32),
            jax.ShapeDtypeStruct((devices, HD), F32),
        ),
        compiler_params=pltpu.CompilerParams(vmem_limit_bytes=24 * 1024 * 1024),
        name="sum_gradient",
    )(parts)


def update_kernel(
    squares_ref, gradient_ref, state_ref, weight_ref, step_ref, rollout_ref, *, entries
):
    squares = jnp.sum(squares_ref[...], axis=0, keepdims=True)[:, :1]
    factor = jnp.minimum(1.0, clip_rms / jnp.sqrt(squares / entries + norm_eps))
    rows = weight_ref.shape[0]
    new_weight, adam_step = adamw_update(
        state_ref[:rows],
        gradient_ref[...],
        state_ref[rows : 2 * rows],
        state_ref[2 * rows :],
        factor,
    )
    weight_ref[...] = new_weight
    step_ref[...] = adam_step
    rollout_ref[...] = new_weight.astype(BF16)


def update(squares, gradient, state, entries):
    own = jax.ShapeDtypeStruct(gradient.shape, F32)
    return pl.pallas_call(
        functools.partial(update_kernel, entries=entries),
        out_shape=(own, own, jax.ShapeDtypeStruct(gradient.shape, BF16)),
        compiler_params=pltpu.CompilerParams(vmem_limit_bytes=24 * 1024 * 1024),
        name="update",
    )(squares, gradient, state)


def project_kernel(hidden_ref, *refs):
    weights = jnp.concatenate([ref[...] for ref in refs[:-1]])
    partial = jnp.dot(hidden_ref[...], weights, preferred_element_type=F32)
    refs[-1][...] = partial.astype(BF16)


def project(hidden, weights):
    return pl.pallas_call(
        project_kernel,
        out_shape=jax.ShapeDtypeStruct((hidden.shape[0], weights[0].shape[1]), BF16),
        compiler_params=pltpu.CompilerParams(vmem_limit_bytes=24 * 1024 * 1024),
        name="project",
    )(hidden, *weights)


def local(
    tokens,
    grad_out,
    weight,
    moment_one,
    moment_two,
    rollout_hidden,
    queries,
    cache_keys,
    cache_values,
    cache_lengths,
    key_gain,
):
    token_count = tokens.shape[0]
    total_tokens = token_count * 64
    own_rows = weight.shape[0]
    columns = weight.shape[1] * weight.shape[2]
    entry_count = own_rows * 64 * columns * 4
    z = lax.axis_index("z")
    xl = lax.axis_index("xl")
    xh = lax.axis_index("xh")
    core = lax.axis_index("core")

    with jax.named_scope("exchange"):
        upstream_other = swap(grad_out, "xh")
        tokens_other = swap(tokens, "core")
        upstream = grad_out.reshape(token_count, columns)

    row_count, step_count, model_width = rollout_hidden.shape
    states = row_count * step_count
    head_count = weight.shape[2] // HD
    groups = QH // KVH

    def by_xl(first, second):
        def slots(at):
            return jnp.stack(
                [lax.dynamic_index_in_dim(block, at, keepdims=False) for block in (first, second)]
            )

        return slots(xl), slots(1 - xl)

    def in_order(block):
        return jnp.where(core == 0, block, block[::-1]).reshape(4, own_rows, columns)

    def from_y(values, step):
        return lax.ppermute(values, "y", [(a, a ^ step) for a in range(4)])

    def trade(block, axis, bit, partners):
        mesh_axis = "xl" if bit is None else "z"
        mine = xl if bit is None else (z >> bit) & 1
        kept = lax.dynamic_index_in_dim(block, mine, axis=axis, keepdims=False)
        sent = lax.dynamic_index_in_dim(block, 1 - mine, axis=axis, keepdims=False)
        got = lax.ppermute(sent, mesh_axis, partners)
        return jnp.where(
            mine == 0, jnp.stack([kept, got], axis=axis), jnp.stack([got, kept], axis=axis)
        )

    def trade_z(block, bit):
        return trade(block, 2 - bit, bit, [(a, a ^ (1 << bit)) for a in range(8)])

    with jax.named_scope("first_half"):
        away, one_near, one_mine = product(tokens, upstream, 0, own_rows)
        away, tokens_other, queries, rollout_hidden = together(
            away, tokens_other, queries, rollout_hidden
        )
        one_got = along_y(away, 0)
    with jax.named_scope("hidden"):
        hidden = rollout_hidden.reshape(states, 16, 4 * own_rows).transpose(1, 0, 2)
        hidden = hidden.reshape(2, 2, 2, 2, states, 4 * own_rows)
        hidden = trade_z(hidden, 0)
    with jax.named_scope("first_half"):
        away, two_near, two_mine = product(tokens_other, upstream, 1, own_rows)
        two_near, hidden, weight, moment_one, moment_two = together(
            two_near, hidden, weight, moment_one, moment_two
        )
        two_got = along_y(away, 1)
    with jax.named_scope("hidden"):
        hidden = trade_z(trade_z(hidden, 1), 2)
        hidden, upstream_other = together(hidden, upstream_other)
    with jax.named_scope("state"):
        query_heads = queries.reshape(row_count, step_count, head_count, groups, HD)
        query_heads = query_heads.transpose(2, 0, 3, 1, 4)
        query_heads = query_heads.reshape(head_count, row_count, groups * step_count, HD)
        state = jnp.concatenate([weight, moment_one, moment_two]).reshape(3 * own_rows, columns)
    with jax.named_scope("first_half"):
        upstream_other = upstream_other.reshape(token_count, columns)
        one_got, two_got, hidden, query_heads, state, upstream_other = together(
            one_got, two_got, hidden, query_heads, state, upstream_other
        )
        one_passed = add(one_near, one_got[0])
        one_passed, upstream_other = together(one_passed, upstream_other)
        one_last = along_y(one_passed, 1)
    with jax.named_scope("second_half"):
        away, three_near, three_mine = product(tokens, upstream_other, 0, own_rows)
        away, tokens_other, two_near = together(away, tokens_other, two_near)
        three_got = along_y(away, 0)
    with jax.named_scope("first_half"):
        two_passed = add(two_near, two_got[0])
        two_passed, tokens_other = together(two_passed, tokens_other)
        two_last = along_y(two_passed, 0)
    with jax.named_scope("second_half"):
        away, four_near, four_mine = product(tokens_other, upstream_other, 1, own_rows)
        away, one_last, two_last = together(away, one_last, two_last)
        four_got = along_y(away, 1)
    with jax.named_scope("first_half"):
        kept, sent = by_xl(add(one_mine, one_got[1], one_last), add(two_mine, two_got[1], two_last))
        sent, query_heads = together(sent, query_heads)
        arrived = swap(sent, "xl")
    with jax.named_scope("old"):
        old = old_attention(query_heads, cache_keys, cache_values, cache_lengths)
        three_got, *old = together(three_got, *old)
    with jax.named_scope("second_half"):
        three_passed = add(three_near, three_got[0])
        four_passed = add(four_near, four_got[0])
        three_passed, four_passed, arrived = together(three_passed, four_passed, arrived)
        three_last = along_y(three_passed, 1)
        four_last = along_y(four_passed, 0)
    with jax.named_scope("first_half"):
        first = in_order(add(kept, arrived))
    with jax.named_scope("second_half"):
        three_last, first = together(three_last, first)
        kept, sent = by_xl(
            add(three_mine, three_got[1], three_last), add(four_mine, four_got[1], four_last)
        )
        second = in_order(add(kept, swap(sent, "xl")))
    with jax.named_scope("reduce_z"):
        parts = jnp.where(
            xh == 0, jnp.concatenate([first, second]), jnp.concatenate([second, first])
        )
        parts = lax.all_to_all(parts, "z", 0, 0)
        gradient, squares = sum_gradient(parts, total_tokens, 256)
        gradient, squares, hidden = together(gradient, squares, hidden)
    with jax.named_scope("hidden"):
        hidden = trade(hidden, 3, None, [(0, 1), (1, 0)])
        y = lax.axis_index("y")
        hidden = hidden.reshape(16 * states, 4, own_rows)
        hidden = jnp.concatenate(
            [
                lax.dynamic_index_in_dim(hidden, y ^ step, axis=1, keepdims=False)
                for step in range(4)
            ],
            axis=1,
        )
    with jax.named_scope("squares"):
        squares = lax.all_to_all(squares, EVERY, 0, 0, tiled=True)
    with jax.named_scope("place"):
        pairs = [(a * 2 + b, (a + 4) % 8 * 2 + 1 - b) for a in range(8) for b in range(2) if a // 4 != b]
        placed = lax.ppermute(gradient, ("z", "xh"), pairs)
        gradient = jnp.where(z // 4 == xh, gradient, placed)
        gradient, squares, hidden = together(gradient, squares, hidden)
    with jax.named_scope("update"):
        new_weight, adam_step, rollout_weight = update(
            squares, gradient, state, float(entry_count)
        )
    with jax.named_scope("project"):
        weights = [rollout_weight] + [from_y(rollout_weight, step) for step in range(1, 4)]
        partial = project(hidden, weights)
        partial = lax.all_to_all(partial.reshape(16, states, columns), ("z", "xl"), 0, 0)
    with jax.named_scope("angles"):
        half_width = HD // 2
        frequency = rope_base ** (-2.0 * jnp.arange(half_width, dtype=F32) / HD)
        positions = cache_lengths[:, None] + jnp.arange(step_count, dtype=jnp.int32)[None, :]
        angles = positions.astype(F32).reshape(states, 1) * frequency
        cosine = jnp.cos(angles)
        sine = jnp.sin(angles)
        cosine = jnp.concatenate([cosine, cosine], axis=-1)
        sine = jnp.concatenate([-sine, sine], axis=-1)
    with jax.named_scope("fresh"):
        new_keys, new_values, attended = fresh_attention(
            partial,
            *[
                values.reshape(head_count, groups * states, HD)
                for values in (query_heads, *old)
            ],
            key_gain.reshape(1, HD),
            cosine,
            sine,
            step_count,
        )
    return (
        new_weight.reshape(own_rows, 2, columns // 2),
        adam_step.reshape(own_rows, 2, columns // 2),
        new_keys,
        new_values,
        attended,
    )


def solution(mesh):
    fine = Mesh(mesh.devices.reshape(tuple(SIZES.values())), tuple(SIZES))
    in_specs = (
        P(FSDP, TP),
        P(FSDP, None, TP),
        P(FSDP, None, TP),
        P(FSDP, None, TP),
        P(FSDP, None, TP),
        P(FSDP, None, None),
        P(FSDP, None, TP),
        P(FSDP, None, TP),
        P(FSDP, None, TP),
        P(FSDP),
        P(),
    )
    out_specs = (P(FSDP, None, TP),) * 5
    return jax.shard_map(local, mesh=fine, in_specs=in_specs, out_specs=out_specs, check_vma=False)
```

```python
import functools
import math

import jax
import jax.numpy as jnp
from jax import lax
from jax.experimental import pallas as pl
from jax.experimental.pallas import tpu as pltpu
from jax.sharding import Mesh
from jax.sharding import PartitionSpec as P

QH = 64
KVH = 8
HD = 128

beta_one = 0.9
beta_two = 0.999
learn_rate = 0.001
decay_rate = 0.1
adam_eps = 1e-08
step_number = 10.0
clip_rms = 0.001
norm_eps = 1e-06
rope_base = 1000000.0

SIZES = {"z": 8, "xl": 2, "y": 4, "xh": 2, "core": 2}
FSDP = ("z", "xl", "y")
TP = ("xh", "core")
EVERY = FSDP + TP

BF16 = jnp.bfloat16
F32 = jnp.float32


def adamw_update(weight, gradient, moment_one, moment_two, factor):
    clipped = gradient * factor
    first_moment = beta_one * moment_one + (1.0 - beta_one) * clipped
    second_moment = beta_two * moment_two + (1.0 - beta_two) * clipped * clipped
    first_hat = first_moment / (1.0 - beta_one**step_number)
    second_hat = second_moment / (1.0 - beta_two**step_number)
    direction = first_hat / (jnp.sqrt(second_hat) + adam_eps) + decay_rate * weight
    return (weight - learn_rate * direction, direction)


def swap(values, axis):
    return lax.ppermute(values, axis, [(0, 1), (1, 0)])


PAIRING = ([(0, 1), (1, 0), (2, 3), (3, 2)], [(0, 3), (3, 0), (1, 2), (2, 1)])


def partner(position, pairing):
    return position ^ 1 if pairing == 0 else 3 - position


def in_hbm(values):
    return pltpu.with_memory_space_constraint(values, pltpu.HBM)


def product_kernel(order, left_ref, right_ref, away_ref, near_ref, mine_ref, total_ref):
    total_ref[...] = lax.dot_general(
        left_ref[...], right_ref[...], (((0,), (0,)), ((), ())), preferred_element_type=F32
    )
    rows = mine_ref.shape[2]
    for x in range(2):
        for slot in range(4):
            at = pl.multiple_of((x * 4 + order[slot]) * rows, rows)
            block = total_ref[pl.ds(at, rows), :].astype(BF16)
            if slot < 2:
                away_ref[slot, x, 0] = block
            elif slot == 2:
                near_ref[x, 0] = block
            else:
                mine_ref[x, 0] = block


def product(left, right, pairing, rows):
    tokens, columns = right.shape
    me = lax.axis_index("y")
    far = partner(me, pairing)
    near = partner(me, 1 - pairing)
    order = jnp.stack([partner(far, 1 - pairing), far, near, me]).astype(jnp.int32)
    part = pltpu.HBM((2, 2, rows, columns), BF16)
    part_spec = pl.BlockSpec((2, 1, rows, columns), lambda k, order: (0, k, 0, 0))
    return pl.pallas_call(
        product_kernel,
        out_shape=(pltpu.HBM((2, 2, 2, rows, columns), BF16), part, part),
        grid_spec=pltpu.PrefetchScalarGridSpec(
            num_scalar_prefetch=1,
            grid=(2,),
            in_specs=[
                pl.BlockSpec((tokens, 8 * rows), lambda k, order: (0, k)),
                pl.BlockSpec((tokens, columns), lambda k, order: (0, 0)),
            ],
            out_specs=[
                pl.BlockSpec((2, 2, 1, rows, columns), lambda k, order: (0, 0, k, 0, 0)),
                part_spec,
                part_spec,
            ],
            scratch_shapes=[pltpu.VMEM((8 * rows, columns), F32)],
        ),
        compiler_params=pltpu.CompilerParams(vmem_limit_bytes=24 * 1024 * 1024),
        name="product",
    )(order, in_hbm(left), right)


def add(*values):
    total = values[0].astype(F32)
    for value in values[1:]:
        total = total + value.astype(F32)
    return total.astype(BF16)


def along_y(values, pairing):
    return lax.ppermute(values, "y", PAIRING[pairing])


def together(*values):
    return lax.optimization_barrier(values)


def old_attention_kernel(length_ref, query_ref, key_ref, value_ref, out_ref, top_ref, total_ref):
    length = length_ref[pl.program_id(0)]
    scores = lax.dot_general(
        query_ref[0, 0], key_ref[0], (((1,), (1,)), ((), ())), preferred_element_type=F32
    ) * (1.0 / math.sqrt(HD))
    slot = lax.broadcasted_iota(jnp.int32, scores.shape, 1)
    scores = jnp.where(slot < length, scores, -jnp.inf)
    top = jnp.max(scores, axis=-1, keepdims=True)
    weights = jnp.exp(scores - top)
    total = jnp.sum(weights, axis=-1, keepdims=True)
    out_ref[0, 0] = jnp.dot(weights.astype(BF16), value_ref[0], preferred_element_type=F32)
    top_ref[0, 0] = jnp.broadcast_to(top, top_ref.shape[2:])
    total_ref[0, 0] = jnp.broadcast_to(total, total_ref.shape[2:])


def old_attention(query_heads, cache_keys, cache_values, cache_lengths):
    heads, rows, queries, _ = query_heads.shape
    cache = cache_keys.shape[1]
    small = pl.BlockSpec((1, 1, queries, HD), lambda r, h, lengths: (h, r, 0, 0))
    large = pl.BlockSpec((1, cache, HD), lambda r, h, lengths: (r, 0, h))
    shape = jax.ShapeDtypeStruct((heads, rows, queries, HD), F32)
    return pl.pallas_call(
        old_attention_kernel,
        out_shape=(shape, shape, shape),
        grid_spec=pltpu.PrefetchScalarGridSpec(
            num_scalar_prefetch=1,
            grid=(rows, heads),
            in_specs=[small, large, large],
            out_specs=[small, small, small],
        ),
        compiler_params=pltpu.CompilerParams(vmem_limit_bytes=24 * 1024 * 1024),
        name="old_attention",
    )(cache_lengths, query_heads, in_hbm(cache_keys), in_hbm(cache_values))


def fresh_kernel(
    part_ref,
    query_ref,
    old_sum_ref,
    old_top_ref,
    old_total_ref,
    gain_ref,
    cosine_ref,
    sine_ref,
    keys_ref,
    values_ref,
    attended_ref,
    mixed_ref,
    *,
    steps,
):
    heads, queries, _ = query_ref.shape
    states = part_ref.shape[1]
    groups = queries // states
    projected = jnp.sum(part_ref[...].astype(F32), axis=0)
    query = lax.broadcasted_iota(jnp.int32, (queries, states), 0)
    key = lax.broadcasted_iota(jnp.int32, (queries, states), 1)
    row_queries = groups * steps
    valid = (query // row_queries == key // steps) & (query % steps >= key % steps)
    for head in range(heads):
        at = slice(head * HD, (head + 1) * HD)
        raw = projected[:, at]
        mean = jnp.mean(raw * raw, axis=-1, keepdims=True)
        normed = raw * lax.rsqrt(mean + norm_eps) * gain_ref[...]
        turned = normed * cosine_ref[...] + pltpu.roll(normed, HD // 2, 1) * sine_ref[...]
        keys = turned.astype(BF16)
        raw_values = projected[:, heads * HD + head * HD : heads * HD + (head + 1) * HD]
        values = raw_values.astype(BF16)
        for row in range(states // steps):
            own = slice(row * steps, (row + 1) * steps)
            keys_ref[row, :, at] = turned[own].astype(BF16)
            values_ref[row, :, at] = raw_values[own].astype(BF16)
        scores = lax.dot_general(
            query_ref[head], keys, (((1,), (1,)), ((), ())), preferred_element_type=F32
        ) * (1.0 / math.sqrt(HD))
        scores = jnp.where(valid, scores, -jnp.inf)
        old_top = old_top_ref[head]
        top = jnp.maximum(old_top, jnp.max(scores, axis=-1, keepdims=True))
        exps = jnp.exp(scores - top[:, :1])
        old_scale = jnp.exp(old_top - top)
        inverse = 1.0 / (old_total_ref[head] * old_scale + jnp.sum(exps, axis=-1, keepdims=True))
        weights = (exps * inverse[:, :1]).astype(BF16)
        mixed = old_sum_ref[head] * (old_scale * inverse)
        mixed = mixed + jnp.dot(weights, values, preferred_element_type=F32)
        for row in range(states // steps):
            for group in range(groups):
                column = (head * groups + group) * HD
                source = row * row_queries + group * steps
                mixed_ref[row * steps : (row + 1) * steps, column : column + HD] = mixed[
                    source : source + steps
                ]
    for row in range(states // steps):
        attended_ref[row] = mixed_ref[row * steps : (row + 1) * steps].astype(BF16)


def fresh_attention(parts, query_heads, old_sum, old_top, old_total, key_gain, cosine, sine, steps):
    heads, queries, _ = query_heads.shape
    states = parts.shape[1]
    return pl.pallas_call(
        functools.partial(fresh_kernel, steps=steps),
        out_shape=(
            jax.ShapeDtypeStruct((states // steps, steps, heads * HD), BF16),
            jax.ShapeDtypeStruct((states // steps, steps, heads * HD), BF16),
            jax.ShapeDtypeStruct((states // steps, steps, heads * queries // states * HD), BF16),
        ),
        scratch_shapes=[pltpu.VMEM((states, heads * queries // states * HD), F32)],
        compiler_params=pltpu.CompilerParams(vmem_limit_bytes=24 * 1024 * 1024),
        name="fresh_attention",
    )(parts, query_heads, old_sum, old_top, old_total, key_gain, cosine, sine)


def gradient_kernel(parts_ref, gradient_ref, squares_ref, *, total_tokens):
    gradient = jnp.sum(parts_ref[...].astype(F32), axis=0) / total_tokens
    gradient_ref[...] = gradient
    squares_ref[...] = jnp.broadcast_to(jnp.sum(gradient * gradient), squares_ref.shape)


def sum_gradient(parts, total_tokens, devices):
    return pl.pallas_call(
        functools.partial(gradient_kernel, total_tokens=total_tokens),
        out_shape=(
            jax.ShapeDtypeStruct(parts.shape[1:], F32),
            jax.ShapeDtypeStruct((devices, HD), F32),
        ),
        compiler_params=pltpu.CompilerParams(vmem_limit_bytes=24 * 1024 * 1024),
        name="sum_gradient",
    )(parts)


def update_kernel(
    squares_ref, gradient_ref, state_ref, weight_ref, step_ref, rollout_ref, *, entries
):
    squares = jnp.sum(squares_ref[...], axis=0, keepdims=True)[:, :1]
    factor = jnp.minimum(1.0, clip_rms / jnp.sqrt(squares / entries + norm_eps))
    rows = weight_ref.shape[0]
    new_weight, adam_step = adamw_update(
        state_ref[:rows],
        gradient_ref[...],
        state_ref[rows : 2 * rows],
        state_ref[2 * rows :],
        factor,
    )
    weight_ref[...] = new_weight
    step_ref[...] = adam_step
    rollout_ref[...] = new_weight.astype(BF16)


def update(squares, gradient, state, entries):
    own = jax.ShapeDtypeStruct(gradient.shape, F32)
    return pl.pallas_call(
        functools.partial(update_kernel, entries=entries),
        out_shape=(own, own, jax.ShapeDtypeStruct(gradient.shape, BF16)),
        compiler_params=pltpu.CompilerParams(vmem_limit_bytes=24 * 1024 * 1024),
        name="update",
    )(squares, gradient, state)


def project_kernel(hidden_ref, *refs):
    weights = jnp.concatenate([ref[...] for ref in refs[:-1]])
    partial = jnp.dot(hidden_ref[...], weights, preferred_element_type=F32)
    refs[-1][...] = partial.astype(BF16)


def project(hidden, weights):
    return pl.pallas_call(
        project_kernel,
        out_shape=jax.ShapeDtypeStruct((hidden.shape[0], weights[0].shape[1]), BF16),
        compiler_params=pltpu.CompilerParams(vmem_limit_bytes=24 * 1024 * 1024),
        name="project",
    )(hidden, *weights)


def local(
    tokens,
    grad_out,
    weight,
    moment_one,
    moment_two,
    rollout_hidden,
    queries,
    cache_keys,
    cache_values,
    cache_lengths,
    key_gain,
):
    token_count = tokens.shape[0]
    total_tokens = token_count * 64
    own_rows = weight.shape[0]
    columns = weight.shape[1] * weight.shape[2]
    entry_count = own_rows * 64 * columns * 4
    z = lax.axis_index("z")
    xl = lax.axis_index("xl")
    xh = lax.axis_index("xh")
    core = lax.axis_index("core")

    with jax.named_scope("exchange"):
        upstream_other = swap(grad_out, "xh")
        tokens_other = swap(tokens, "core")
        upstream = grad_out.reshape(token_count, columns)

    row_count, step_count, model_width = rollout_hidden.shape
    states = row_count * step_count
    head_count = weight.shape[2] // HD
    groups = QH // KVH

    def by_xl(first, second):
        def slots(at):
            return jnp.stack(
                [lax.dynamic_index_in_dim(block, at, keepdims=False) for block in (first, second)]
            )

        return slots(xl), slots(1 - xl)

    def in_order(block):
        return jnp.where(core == 0, block, block[::-1]).reshape(4, own_rows, columns)

    def from_y(values, step):
        return lax.ppermute(values, "y", [(a, a ^ step) for a in range(4)])

    def trade(block, axis, bit, partners):
        mesh_axis = "xl" if bit is None else "z"
        mine = xl if bit is None else (z >> bit) & 1
        kept = lax.dynamic_index_in_dim(block, mine, axis=axis, keepdims=False)
        sent = lax.dynamic_index_in_dim(block, 1 - mine, axis=axis, keepdims=False)
        got = lax.ppermute(sent, mesh_axis, partners)
        return jnp.where(
            mine == 0, jnp.stack([kept, got], axis=axis), jnp.stack([got, kept], axis=axis)
        )

    def trade_z(block, bit):
        return trade(block, 2 - bit, bit, [(a, a ^ (1 << bit)) for a in range(8)])

    with jax.named_scope("first_half"):
        away, one_near, one_mine = product(tokens, upstream, 0, own_rows)
        away, tokens_other, queries, rollout_hidden = together(
            away, tokens_other, queries, rollout_hidden
        )
        one_got = along_y(away, 0)
    with jax.named_scope("hidden"):
        hidden = rollout_hidden.reshape(states, 16, 4 * own_rows).transpose(1, 0, 2)
        hidden = hidden.reshape(2, 2, 2, 2, states, 4 * own_rows)
        hidden = trade_z(hidden, 0)
    with jax.named_scope("first_half"):
        away, two_near, two_mine = product(tokens_other, upstream, 1, own_rows)
        two_near, hidden, weight, moment_one, moment_two = together(
            two_near, hidden, weight, moment_one, moment_two
        )
        two_got = along_y(away, 1)
    with jax.named_scope("hidden"):
        hidden = trade_z(trade_z(hidden, 1), 2)
        hidden, upstream_other = together(hidden, upstream_other)
    with jax.named_scope("state"):
        query_heads = queries.reshape(row_count, step_count, head_count, groups, HD)
        query_heads = query_heads.transpose(2, 0, 3, 1, 4)
        query_heads = query_heads.reshape(head_count, row_count, groups * step_count, HD)
        state = jnp.concatenate([weight, moment_one, moment_two]).reshape(3 * own_rows, columns)
    with jax.named_scope("first_half"):
        upstream_other = upstream_other.reshape(token_count, columns)
        one_got, two_got, hidden, query_heads, state, upstream_other = together(
            one_got, two_got, hidden, query_heads, state, upstream_other
        )
        one_passed = add(one_near, one_got[0])
        two_passed = add(two_near, two_got[0])
        one_passed, two_passed, upstream_other = together(one_passed, two_passed, upstream_other)
        one_last = along_y(one_passed, 1)
        two_last = along_y(two_passed, 0)
    with jax.named_scope("second_half"):
        away, three_near, three_mine = product(tokens, upstream_other, 0, own_rows)
        away, tokens_other = together(away, tokens_other)
        three_got = along_y(away, 0)
        away, four_near, four_mine = product(tokens_other, upstream_other, 1, own_rows)
        away, one_last, two_last = together(away, one_last, two_last)
        four_got = along_y(away, 1)
    with jax.named_scope("first_half"):
        kept, sent = by_xl(add(one_mine, one_got[1], one_last), add(two_mine, two_got[1], two_last))
        sent, query_heads = together(sent, query_heads)
        arrived = swap(sent, "xl")
    with jax.named_scope("old"):
        old = old_attention(query_heads, cache_keys, cache_values, cache_lengths)
        three_got, *old = together(three_got, *old)
    with jax.named_scope("second_half"):
        three_passed = add(three_near, three_got[0])
        four_passed = add(four_near, four_got[0])
        three_passed, four_passed, arrived = together(three_passed, four_passed, arrived)
        three_last = along_y(three_passed, 1)
        four_last = along_y(four_passed, 0)
    with jax.named_scope("first_half"):
        first = in_order(add(kept, arrived))
    with jax.named_scope("second_half"):
        three_last, first = together(three_last, first)
        kept, sent = by_xl(
            add(three_mine, three_got[1], three_last), add(four_mine, four_got[1], four_last)
        )
        second = in_order(add(kept, swap(sent, "xl")))
    with jax.named_scope("reduce_z"):
        parts = jnp.where(
            xh == 0, jnp.concatenate([first, second]), jnp.concatenate([second, first])
        )
        parts = lax.all_to_all(parts, "z", 0, 0)
        gradient, squares = sum_gradient(parts, total_tokens, 256)
        gradient, squares, hidden = together(gradient, squares, hidden)
    with jax.named_scope("hidden"):
        hidden = trade(hidden, 3, None, [(0, 1), (1, 0)])
        y = lax.axis_index("y")
        hidden = hidden.reshape(16 * states, 4, own_rows)
        hidden = jnp.concatenate(
            [
                lax.dynamic_index_in_dim(hidden, y ^ step, axis=1, keepdims=False)
                for step in range(4)
            ],
            axis=1,
        )
    with jax.named_scope("squares"):
        squares = lax.all_to_all(squares, EVERY, 0, 0, tiled=True)
    with jax.named_scope("place"):
        pairs = [(a * 2 + b, (a + 4) % 8 * 2 + 1 - b) for a in range(8) for b in range(2) if a // 4 != b]
        placed = lax.ppermute(gradient, ("z", "xh"), pairs)
        gradient = jnp.where(z // 4 == xh, gradient, placed)
        gradient, squares, hidden = together(gradient, squares, hidden)
    with jax.named_scope("update"):
        new_weight, adam_step, rollout_weight = update(
            squares, gradient, state, float(entry_count)
        )
    with jax.named_scope("project"):
        weights = [rollout_weight] + [from_y(rollout_weight, step) for step in range(1, 4)]
        partial = project(hidden, weights)
        partial = lax.all_to_all(partial.reshape(16, states, columns), ("z", "xl"), 0, 0)
    with jax.named_scope("angles"):
        half_width = HD // 2
        frequency = rope_base ** (-2.0 * jnp.arange(half_width, dtype=F32) / HD)
        positions = cache_lengths[:, None] + jnp.arange(step_count, dtype=jnp.int32)[None, :]
        angles = positions.astype(F32).reshape(states, 1) * frequency
        cosine = jnp.cos(angles)
        sine = jnp.sin(angles)
        cosine = jnp.concatenate([cosine, cosine], axis=-1)
        sine = jnp.concatenate([-sine, sine], axis=-1)
    with jax.named_scope("fresh"):
        new_keys, new_values, attended = fresh_attention(
            partial,
            *[
                values.reshape(head_count, groups * states, HD)
                for values in (query_heads, *old)
            ],
            key_gain.reshape(1, HD),
            cosine,
            sine,
            step_count,
        )
    return (
        new_weight.reshape(own_rows, 2, columns // 2),
        adam_step.reshape(own_rows, 2, columns // 2),
        new_keys,
        new_values,
        attended,
    )


def solution(mesh):
    fine = Mesh(mesh.devices.reshape(tuple(SIZES.values())), tuple(SIZES))
    in_specs = (
        P(FSDP, TP),
        P(FSDP, None, TP),
        P(FSDP, None, TP),
        P(FSDP, None, TP),
        P(FSDP, None, TP),
        P(FSDP, None, None),
        P(FSDP, None, TP),
        P(FSDP, None, TP),
        P(FSDP, None, TP),
        P(FSDP),
        P(),
    )
    out_specs = (P(FSDP, None, TP),) * 5
    return jax.shard_map(local, mesh=fine, in_specs=in_specs, out_specs=out_specs, check_vma=False)
```
